512 devices in a mesh: row: 32 (over x_lo, z), col: 16 (over x_hi, y, core).
Axes of the slice: x: 4 (x_hi: 2, x_lo: 2; x = x_hi * 2 + x_lo), y: 4, z: 16, core: 2. Of those that a mesh axis runs over, the one named last changes fastest.
Arguments:
- train_codes: bfloat16 [16384, 32768], P('row', 'col'), may hold values from -6 to 6
- train_exps: int32 [16384, 256], P('row', 'col'), may hold values from -3 to 3
- train_ids: int32 [16384], P('row'), may hold values from 0 to 63
- query_codes: bfloat16 [2048, 32768], P('row', 'col'), may hold values from -6 to 6
- query_exps: int32 [2048, 256], P('row', 'col'), may hold values from -3 to 3
- query_ids: int32 [2048], P('row'), may hold values from 0 to 63
- precond: float32 [32768], P('col'), may hold values from 0.1 to 10
Outputs:
- cosines: float32 [16384, 2048], P('row', 'col')
- peak: float32 [16384], P('row')
The draws below stay inside these ranges and needn't reach their ends.
All inputs are finite; a program needn't handle non-finite values.
Results may differ from the reference program's by a relative error of at most 0.0045.
Values may be sent and summed in bfloat16 or wider, within the bound.
A program may use at most 64 MiB of HBM per device.

```python
import math
import jax
import jax.numpy as jnp
from jax import lax

P_SIZE = 32768
BLOCK = 128
DOCS = 64
TR_DEV = 512
NTRAIN = 16384
NQ = 2048
N_ROW = 32


def touch_ends(array, stream_key, least, largest):
    longest = array.shape.index(max(array.shape))
    spots = []
    for shift in (0, 1):
        where = [jax.random.randint(jax.random.fold_in(stream_key, axis), (), 0, length) for axis, length in enumerate(array.shape)]
        where[longest] = (where[longest] + shift) % array.shape[longest]
        spots.append(tuple(where))
    return array.at[spots[0]].set(least).at[spots[1]].set(largest)


def shard_levels(own_key, extent, cuts, least, top_value):
    level = 1.0
    for position, blocks in cuts:
        steps = jax.random.uniform(jax.random.fold_in(jax.random.fold_in(own_key, 6), position), (blocks,), jnp.float32, least / len(cuts), top_value / len(cuts))
        level = level * jnp.repeat(jnp.exp(steps), extent[position] // blocks).reshape((-1,) + (1,) * (len(extent) - 1 - position))
    return level


def noise(key, shape, spread, limit, shards=(), held_as=jnp.bfloat16):
    drawn = jax.random.normal(key, shape, jnp.float32) * spread
    if len(shards) > 0:
        drawn = shard_levels(key, shape, shards, -0.22, 0.18) * drawn
    return jnp.clip(drawn, min=-limit, max=limit).astype(held_as)


def setup_inputs(seed: int = 0) -> dict:
    key_of = jax.random.split(jax.random.key(seed), 8)
    train_codes = noise(key_of[0], (NTRAIN, P_SIZE), 1.0, 6.0, ((0, 32), (1, 16)))
    train_exps = touch_ends(jax.random.randint(key_of[1], (NTRAIN, P_SIZE // BLOCK), -3, 4), jax.random.fold_in(key_of[1], 1), -3, 3).astype(jnp.int32)
    train_ids = touch_ends(jax.random.randint(key_of[2], (NTRAIN,), 0, DOCS), jax.random.fold_in(key_of[2], 1), 0, DOCS - 1).astype(jnp.int32)
    query_codes = noise(key_of[3], (NQ, P_SIZE), 1.0, 6.0, ((0, 32), (1, 16)))
    query_exps = touch_ends(jax.random.randint(key_of[4], (NQ, P_SIZE // BLOCK), -3, 4), jax.random.fold_in(key_of[4], 1), -3, 3).astype(jnp.int32)
    query_ids = touch_ends(jax.random.randint(key_of[5], (NQ,), 0, DOCS), jax.random.fold_in(key_of[5], 1), 0, DOCS - 1).astype(jnp.int32)
    precond = jnp.clip(jnp.exp(math.log(10.0) - 4.6051702 * jax.random.uniform(key_of[6], (P_SIZE,), jnp.float32) ** shard_levels(key_of[6], (P_SIZE,), ((0, 16),), -0.2, 0.2)), 0.1, 10.0)
    return dict(train_codes=train_codes, train_exps=train_exps, train_ids=train_ids, query_codes=query_codes, query_exps=query_exps, query_ids=query_ids, precond=precond)


epsilon = 1e-06

def dequantize(codes, exps):
    count = codes.shape[0]
    blocks = exps.shape[1]
    factor = jnp.exp2(exps.astype(jnp.float32)).astype(jnp.bfloat16)
    shaped = codes.reshape(count, blocks, codes.shape[1] // blocks) * factor[:, :, None]
    return shaped.reshape(count, codes.shape[1])

def precondition(codes, exps, precond):
    count = codes.shape[0]
    blocks = exps.shape[1]
    factor = jnp.exp2(exps.astype(jnp.float32))
    shaped = codes.astype(jnp.float32).reshape(count, blocks, codes.shape[1] // blocks) * factor[:, :, None]
    return (shaped.reshape(count, codes.shape[1]) * precond[None, :]).astype(jnp.bfloat16)

def squares(values):
    return lax.optimization_barrier(jnp.sum(jnp.square(values.astype(jnp.float32)), axis=1))

def reference(train_codes, train_exps, train_ids, query_codes, query_exps, query_ids, precond):
    query_pre = precondition(query_codes, query_exps, precond)
    query_sq = squares(query_pre)
    scale = math.sqrt(P_SIZE)

    def one_block(pieces):
        codes, exps, ids = pieces
        train_grad = dequantize(codes, exps)
        train_sq = squares(train_grad)
        raw = jnp.dot(train_grad, query_pre.T, preferred_element_type=jnp.float32)
        denom = jnp.sqrt((train_sq[:, None] + epsilon) * (query_sq[None, :] + epsilon))
        similar = jnp.where(ids[:, None] == query_ids[None, :], jnp.float32(0.0), scale * raw / denom)
        return (similar, lax.optimization_barrier(jnp.max(similar, axis=1)))
    blocks_in = (train_codes.reshape(N_ROW, TR_DEV, P_SIZE), train_exps.reshape(N_ROW, TR_DEV, P_SIZE // BLOCK), train_ids.reshape(N_ROW, TR_DEV))
    cosines, peak = lax.map(one_block, blocks_in)
    return (cosines.reshape(NTRAIN, NQ), peak.reshape(NTRAIN))
```

```python
import functools
import math

import jax
import jax.numpy as jnp
from jax import lax
from jax.experimental import pallas as pl
from jax.experimental.pallas import tpu as pltpu
from jax.sharding import PartitionSpec as P

P_SIZE = 32768
EPS = 1e-06
MESH = pl.DeviceIdType.MESH
F32 = jnp.float32
BF16 = jnp.bfloat16

NZ = 16
BLK = 64
KD = 2048
ROWS = 512
LANES = 128
NBLK = KD // LANES
NCH = 4
CH = BLK // NCH
XCH = 64
NX = ROWS // XCH


def dist(a, b):
    return jnp.minimum((a - b + NZ) % NZ, (b - a + NZ) % NZ)


def slot_of(z, block):
    first = (block // 2) * 2
    last = jnp.maximum(dist(z, first), dist(z, first + 1))
    return (last - 1) * 2 + block % 2


def pair_of(z, step):
    odd = (z + step) % 2
    return jnp.where(odd == 1, ((z + step) % NZ) // 2, ((z - step + NZ) % NZ) // 2)


def power(exps):
    return lax.shift_left(jnp.int32(1), exps + 3).astype(F32) * 0.125


def rcopy(src, dst, send, recv, device):
    return pltpu.make_async_remote_copy(
        src_ref=src, dst_ref=dst, send_sem=send, recv_sem=recv, device_id=device, device_id_type=MESH
    )


def kernel(
    tc_hbm, te_hbm, tid_ref, qc_hbm, qe_ref, qid_ref, pre_ref,
    cos_ref, peak_ref,
    tcode, texp, qcode, a_all, b_all, tsq, s1, r1, loc, s2, r2, acc, sx, rx, keep,
    mine, parts, meta, metas, tinv, tidb, ppart, peaks,
    in_sem, z_send, z_recv, x_send, x_recv, s1_send, s1_recv, s2_send, s2_recv,
    s3_send, s3_recv, a_send, a_recv, m_send, m_recv, p_send, p_recv,
):
    r, c = lax.axis_index("row"), lax.axis_index("col")
    xlo, z = r // NZ, r % NZ
    xhi, y, core = c // 8, (c // 2) % 4, c % 2
    up = (xlo * NZ + (z + 1) % NZ, c)
    down = (xlo * NZ + (z + NZ - 1) % NZ, c)
    xpair = ((1 - xlo) * NZ + z, c)
    xhop = (r, (c + 8) % 16)
    diag = ((1 - xlo) * NZ + z, (c + 8) % 16)
    twin = (r, c + 1 - 2 * core)
    home = xhi == xlo

    barrier = pltpu.get_barrier_semaphore()
    for peer in (up, down, xpair, diag):
        pl.semaphore_signal(barrier, inc=1, device_id=peer, device_id_type=MESH)

    def greet(k, _):
        pl.semaphore_signal(barrier, inc=1, device_id=(r, (c + k) % 16), device_id_type=MESH)
        return 0

    lax.fori_loop(1, 16, greet, 0)
    is_self = [jnp.logical_and(2 * c + i == r, r // 2 == c) for i in range(2)]
    for i in range(2):
        @pl.when(jnp.logical_not(is_self[i]))
        def _():
            pl.semaphore_signal(barrier, inc=1, device_id=(2 * c + i, r // 2), device_id_type=MESH)

    q_in = pltpu.make_async_copy(qc_hbm, qcode, in_sem.at[NX])
    q_in.start()
    e_in = pltpu.make_async_copy(te_hbm, texp, in_sem.at[NX + 1])
    e_in.start()

    def t_in(i):
        rows = pl.ds(i * XCH, XCH)
        return pltpu.make_async_copy(tc_hbm.at[rows], tcode.at[rows], in_sem.at[i])

    for i in range(NX):
        t_in(i).start()

    q_in.wait()
    own = slot_of(z, z) * BLK
    q_factor = power(qe_ref[...])
    qsq = jnp.zeros((BLK, LANES), F32)
    for j in range(NBLK):
        cols = pl.ds(j * LANES, LANES)
        value = (qcode[:, cols].astype(F32) * q_factor[:, j : j + 1] * pre_ref[j : j + 1, :]).astype(BF16)
        b_all[pl.ds(pl.multiple_of(own, BLK), BLK), cols] = value
        qsq += jnp.square(value.astype(F32))

    pl.semaphore_wait(
        barrier, 4 + 15 + 2 - is_self[0].astype(jnp.int32) - is_self[1].astype(jnp.int32)
    )

    def z_rows(zd, block, k):
        return pl.ds(pl.multiple_of(slot_of(zd, block) * BLK + k * CH, CH), CH)

    def z_copy(way, step, k):
        if way == 0:
            block, to, zd = (z - (step - 1) + NZ) % NZ, up, (z + 1) % NZ
        else:
            block, to, zd = (z + (step - 1)) % NZ, down, (z + NZ - 1) % NZ
        return rcopy(
            b_all.at[z_rows(z, block, k)], b_all.at[z_rows(zd, block, k)],
            z_send.at[way, step, k], z_recv.at[way, step, k], to,
        )

    def z_arrival(way, step, k):
        block = (z - step + NZ) % NZ if way == 0 else (z + step) % NZ
        rows = b_all.at[z_rows(z, block, k)]
        return rcopy(rows, rows, z_send.at[way, step, k], z_recv.at[way, step, k], up)

    def chunk_of(way, k):
        return k if way == 0 else (k + NCH // 2) % NCH

    for k in range(NCH):
        for way in range(2):
            z_copy(way, 1, chunk_of(way, k)).start()

    def x_copy(i):
        rows = pl.ds(pl.multiple_of(i * XCH, XCH), XCH)
        there = pl.ds(pl.multiple_of(ROWS + i * XCH, XCH), XCH)
        return rcopy(a_all.at[rows], a_all.at[there], x_send.at[i], x_recv.at[i], xpair)

    e_in.wait()

    def scale(i, _):
        t_in(i).wait()
        rows = pl.ds(pl.multiple_of(i * XCH, XCH), XCH)
        factor = power(texp[rows, :])
        total = jnp.zeros((XCH, LANES), F32)
        for j in range(NBLK):
            cols = pl.ds(j * LANES, LANES)
            value = tcode[rows, cols].astype(F32) * factor[:, j : j + 1]
            a_all[rows, cols] = value.astype(BF16)
            total += jnp.square(value)
        tsq[rows, :] = total

        @pl.when(i < 3)
        def _():
            x_copy(i).start()

        return 0

    lax.fori_loop(0, NX, scale, 0)

    mine[...] = jnp.zeros_like(mine)
    for g in range(4):
        mine[g : g + 1, :] = jnp.sum(tsq[pl.ds(g * LANES, LANES), :].T, axis=0, keepdims=True)
    wide = jnp.concatenate([qsq, jnp.zeros_like(qsq)], axis=0)
    mine[4:5, :] = jnp.sum(wide.T, axis=0, keepdims=True)

    def to_col(src, dst, send, recv, k):
        return rcopy(src, dst.at[c], send.at[k], recv.at[c], (r, (c + k) % 16))

    def from_col(src, dst, send, recv, k):
        who = (c + k) % 16
        return rcopy(src, dst.at[who], send.at[k], recv.at[who], (r, who))

    def send_parts(k, _):
        to_col(mine, parts, a_send, a_recv, k).start()
        return 0

    lax.fori_loop(1, 16, send_parts, 0)
    parts[c] = mine[...]

    def meta_copy(i):
        return rcopy(meta, metas.at[r % 2], m_send.at[i], m_recv.at[r % 2], (2 * c + i, r // 2))

    def norms():
        def got(k, _):
            from_col(mine, parts, a_send, a_recv, k).wait_recv()
            return 0

        lax.fori_loop(1, 16, got, 0)
        total = parts[0]
        for k in range(1, 16):
            total += parts[k]
        scaled = math.sqrt(P_SIZE) / jnp.sqrt(total + EPS)
        ids = tid_ref[...].astype(F32)
        for g in range(4):
            rows = pl.ds(g * LANES, LANES)
            tinv[rows, :] = jnp.broadcast_to(scaled[g : g + 1, :], (LANES, LANES)).T
            tidb[rows, :] = jnp.broadcast_to(ids[g : g + 1, :], (LANES, LANES)).T
        meta[...] = jnp.zeros_like(meta)
        meta[0:1, :] = total[4:5, :]
        meta[1:2, 0:BLK] = qid_ref[...].astype(F32)
        for i in range(2):
            @pl.when(is_self[i])
            def _():
                metas[i] = meta[...]

            @pl.when(jnp.logical_not(is_self[i]))
            def _():
                meta_copy(i).start()

    def big(q):
        return pl.ds(q * 256, 256)

    def small(q):
        return pl.ds(pl.multiple_of(q * LANES + 256, LANES), LANES)

    def hand(value, rows, q, step):
        j = pair_of(z, step)
        cd, yd = j % 2, j // 2

        @pl.when(core != cd)
        def _():
            s1[yd, rows, :] = value
            s1_copy(yd, rows, q).start()

        @pl.when(core == cd)
        def _():
            loc[yd, rows, :] = value

    def s1_copy(yd, rows, q):
        return rcopy(s1.at[yd, rows], r1.at[yd, rows], s1_send.at[yd, q], s1_recv.at[yd, q], twin)

    def s2_copy(yd, rows, q):
        k = (y - yd + 4) % 4 - 1
        return rcopy(
            s2.at[yd, rows], r2.at[k, rows], s2_send.at[yd, q], s2_recv.at[k, q], (r, xhi * 8 + yd * 2 + core)
        )

    def relay(rows, q, step):
        j = pair_of(z, step)
        cd, yd = j % 2, j // 2

        @pl.when(core == cd)
        def _():
            s1_copy(yd, rows, q).wait_recv()
            total = loc[yd, rows, :] + r1[yd, rows, :]

            @pl.when(y == yd)
            def _():
                acc[rows, :] = total

            @pl.when(y != yd)
            def _():
                s2[yd, rows, :] = total.astype(BF16)
                s2_copy(yd, rows, q).start()

    def dot(rows, cols):
        return lax.dot_general(
            a_all[rows, :], b_all[cols, :], (((1,), (1,)), ((), ())), preferred_element_type=F32
        )

    def q_at(step):
        return pl.ds(pl.multiple_of((step - 1) * LANES, LANES), LANES)

    def work_own(step, q):
        hand(dot(big(q), q_at(step)), big(q), q, step)

    def work_old(step):
        def one(q, _):
            hand(dot(small(q), q_at(step)), small(q), q, step)
            return 0

        lax.fori_loop(2, 2 + (step - 1) // 2, one, 0)

    def work_new(step):
        @pl.when(step % 2 == 0)
        def _():
            q = 1 + step // 2
            for i in (step - 2, step - 1):
                x_copy(i).wait_recv()

            def two(t, _):
                cols = pl.ds(pl.multiple_of(t * 2 * LANES, 2 * LANES), 2 * LANES)
                value = dot(small(q), cols)
                hand(value[:, :LANES], small(q), q, 2 * t + 1)
                hand(value[:, LANES:], small(q), q, 2 * t + 2)
                return 0

            lax.fori_loop(0, step // 2, two, 0)

    def pass_on(step):
        for q in range(2):
            relay(big(q), q, step)

        def one(q, _):
            relay(small(q), q, step)
            return 0

        lax.fori_loop(2, 2 + (step - 1) // 2, one, 0)

        @pl.when(step % 2 == 0)
        def _():
            q = 1 + step // 2

            def each(t, _):
                relay(small(q), q, t)
                return 0

            lax.fori_loop(1, step + 1, each, 0)

    def arrive(step, k):
        for way in range(2):
            chunk = chunk_of(way, k)

            @pl.when(jnp.logical_or(step < NZ // 2, k < NCH // 2))
            def _():
                z_arrival(way, step, chunk).wait_recv()

            @pl.when(jnp.logical_or(step < NZ // 2 - 1, jnp.logical_and(step == NZ // 2 - 1, k < NCH // 2)))
            def _():
                z_copy(way, step + 1, chunk).start()

    def body(step, _):
        for k in range(NCH):
            arrive(step, k)
            if k == 0:
                @pl.when(step + 2 < NX)
                def _():
                    x_copy(step + 2).start()

                @pl.when(step == 2)
                def _():
                    norms()

            @pl.when(step > 1)
            def _():
                if k < 2:
                    work_own(step - 1, k)
                elif k == 2:
                    work_old(step - 1)
                else:
                    work_new(step - 1)

        @pl.when(step > 2)
        def _():
            pass_on(step - 2)

        return 0

    lax.fori_loop(1, NZ // 2 + 1, body, 0)
    last = NZ // 2
    pass_on(last - 1)
    for q in range(2):
        work_own(last, q)
    work_old(last)
    work_new(last)
    pass_on(last)

    def summed(rows, q):
        total = acc[rows, :]
        for k in range(3):
            rcopy(r2.at[k, rows], r2.at[k, rows], s2_send.at[0, q], s2_recv.at[k, q], twin).wait_recv()
            total += r2[k, rows, :].astype(F32)
        return total

    def s3_own(u):
        rows = pl.ds(u * LANES, LANES)
        return rcopy(sx.at[rows], rx.at[0, rows], s3_send.at[u], s3_recv.at[0, u], xhop)

    def s3_pair(u):
        rows, there = pl.ds(ROWS + u * LANES, LANES), pl.ds(u * LANES, LANES)
        return rcopy(sx.at[rows], rx.at[0, there], s3_send.at[4 + u], s3_recv.at[0, u], xpair)

    def s3_diag(u):
        rows, there = pl.ds(ROWS + u * LANES, LANES), pl.ds(u * LANES, LANES)
        return rcopy(sx.at[rows], rx.at[1, there], s3_send.at[4 + u], s3_recv.at[1, u], diag)

    for q in range(2):
        total = summed(big(q), q)

        @pl.when(home)
        def _():
            keep[big(q), :] = total

        @pl.when(jnp.logical_not(home))
        def _():
            sx[big(q), :] = total.astype(BF16)
            s3_own(2 * q).start()
            s3_own(2 * q + 1).start()

    for u in range(4):
        sx[pl.ds(ROWS + u * LANES, LANES), :] = summed(pl.ds(ROWS + u * LANES, LANES), u + 2).astype(BF16)

        @pl.when(home)
        def _():
            s3_pair(u).start()

        @pl.when(jnp.logical_not(home))
        def _():
            s3_diag(u).start()

    for i in range(2):
        @pl.when(jnp.logical_not(is_self[i]))
        def _():
            rcopy(meta, metas.at[i], m_send.at[i], m_recv.at[i], up).wait_recv()

    lane = lax.broadcasted_iota(jnp.int32, (8, LANES), 1)
    both = jnp.where(lane < BLK, metas[0], pltpu.roll(metas[1], BLK, 1))
    q_inv = 1.0 / jnp.sqrt(both[0:1, :] + EPS)
    q_ids = both[1:2, :]

    ppart[...] = jnp.zeros_like(ppart)
    for u in range(4):
        rows = pl.ds(u * LANES, LANES)

        s3_pair(u).wait_recv()

        @pl.when(jnp.logical_not(home))
        def _():
            s3_diag(u).wait_recv()
            keep[rows, :] = rx[1, rows, :].astype(F32)

        raw = keep[rows, :] + rx[0, rows, :].astype(F32)
        value = raw * tinv[rows, :] * q_inv
        value = jnp.where(tidb[rows, :] == q_ids, 0.0, value)
        cos_ref[rows, :] = value
        ppart[u : u + 1, :] = jnp.max(value.T, axis=0, keepdims=True)

    def send_peaks(k, _):
        to_col(ppart, peaks, p_send, p_recv, k).start()
        return 0

    lax.fori_loop(1, 16, send_peaks, 0)
    peaks[c] = ppart[...]

    def sent(step, _):
        for k in range(NCH):
            for way in range(2):
                z_copy(way, step, k).wait_send()
        return 0

    lax.fori_loop(1, NZ // 2, sent, 0)
    for k in range(NCH // 2):
        for way in range(2):
            z_copy(way, NZ // 2, chunk_of(way, k)).wait_send()

    def x_sent(i, _):
        x_copy(i).wait_send()
        return 0

    lax.fori_loop(0, NX, x_sent, 0)

    def s_sent(yd, _):
        for q in range(2):
            s1_copy(yd, big(q), q).wait_send()

            @pl.when(yd != y)
            def _():
                s2_copy(yd, big(q), q).wait_send()

        for q in range(2, 6):
            s1_copy(yd, small(q), q).wait_send()

            @pl.when(yd != y)
            def _():
                s2_copy(yd, small(q), q).wait_send()

        return 0

    lax.fori_loop(0, 4, s_sent, 0)
    for u in range(4):
        @pl.when(jnp.logical_not(home))
        def _():
            s3_own(u).wait_send()

        s3_pair(u).wait_send()

    for i in range(2):
        @pl.when(jnp.logical_not(is_self[i]))
        def _():
            meta_copy(i).wait_send()

    def col_done(k, _):
        to_col(mine, parts, a_send, a_recv, k).wait_send()
        to_col(ppart, peaks, p_send, p_recv, k).wait_send()
        from_col(ppart, peaks, p_send, p_recv, k).wait_recv()
        return 0

    lax.fori_loop(1, 16, col_done, 0)
    best = peaks[0]
    for k in range(1, 16):
        best = jnp.maximum(best, peaks[k])
    peak_ref[...] = best[0:4, :]


def shards(train_codes, train_exps, train_ids, query_codes, query_exps, query_ids, precond):
    dma = pltpu.SemaphoreType.DMA
    vmem = pl.BlockSpec(memory_space=pltpu.VMEM)
    hbm = pl.BlockSpec(memory_space=pl.ANY)
    cosines, peak = pl.pallas_call(
        kernel,
        out_shape=(jax.ShapeDtypeStruct((ROWS, LANES), F32), jax.ShapeDtypeStruct((4, LANES), F32)),
        in_specs=[hbm, hbm, vmem, hbm, vmem, vmem, vmem],
        out_specs=(vmem, vmem),
        scratch_shapes=[
            pltpu.VMEM((ROWS, KD), BF16),
            pltpu.VMEM((ROWS, NBLK), jnp.int32),
            pltpu.VMEM((BLK, KD), BF16),
            pltpu.VMEM((2 * ROWS, KD), BF16),
            pltpu.VMEM((NZ * BLK, KD), BF16),
            pltpu.VMEM((ROWS, LANES), F32),
            pltpu.VMEM((4, 2 * ROWS, LANES), F32),
            pltpu.VMEM((4, 2 * ROWS, LANES), F32),
            pltpu.VMEM((4, 2 * ROWS, LANES), F32),
            pltpu.VMEM((4, 2 * ROWS, LANES), BF16),
            pltpu.VMEM((3, 2 * ROWS, LANES), BF16),
            pltpu.VMEM((2 * ROWS, LANES), F32),
            pltpu.VMEM((2 * ROWS, LANES), BF16),
            pltpu.VMEM((2, ROWS, LANES), BF16),
            pltpu.VMEM((ROWS, LANES), F32),
            pltpu.VMEM((8, LANES), F32),
            pltpu.VMEM((16, 8, LANES), F32),
            pltpu.VMEM((8, LANES), F32),
            pltpu.VMEM((2, 8, LANES), F32),
            pltpu.VMEM((ROWS, LANES), F32),
            pltpu.VMEM((ROWS, LANES), F32),
            pltpu.VMEM((8, LANES), F32),
            pltpu.VMEM((16, 8, LANES), F32),
            dma((NX + 2,)),
            dma((2, NZ // 2 + 1, NCH)), dma((2, NZ // 2 + 1, NCH)),
            dma((NX,)), dma((NX,)),
            dma((4, 6)), dma((4, 6)),
            dma((4, 6)), dma((3, 6)),
            dma((8,)), dma((2, 4)),
            dma((16,)), dma((16,)),
            dma((2,)), dma((2,)),
            dma((16,)), dma((16,)),
        ],
        compiler_params=pltpu.CompilerParams(
            collective_id=0, has_side_effects=True, vmem_limit_bytes=48 * 2**20
        ),
        cost_estimate=pl.CostEstimate(
            flops=2 * ROWS * 2048 * KD, bytes_accessed=3 * 2**20, transcendentals=0
        ),
    )(
        train_codes, train_exps, train_ids.reshape(4, LANES), query_codes, query_exps,
        query_ids.reshape(1, BLK), precond.reshape(NBLK, LANES),
    )
    return cosines, peak.reshape(ROWS)


def solution(mesh):
    in_specs = (
        P("row", "col"),
        P("row", "col"),
        P("row"),
        P("row", "col"),
        P("row", "col"),
        P("row"),
        P("col"),
    )
    out_specs = (P("row", "col"), P("row"))
    return jax.shard_map(shards, mesh=mesh, in_specs=in_specs, out_specs=out_specs, check_vma=False)
```

```python
import functools
import math

import jax
import jax.numpy as jnp
from jax import lax
from jax.experimental import pallas as pl
from jax.experimental.pallas import tpu as pltpu
from jax.sharding import PartitionSpec as P

P_SIZE = 32768
EPS = 1e-06
MESH = pl.DeviceIdType.MESH
F32 = jnp.float32
BF16 = jnp.bfloat16

NZ = 16
BLK = 64
KD = 2048
ROWS = 512
LANES = 128
NBLK = KD // LANES
NCH = 4
CH = BLK // NCH
XCH = 16
NX = ROWS // XCH
XLEAD = 4
NIN = 8
TCH = ROWS // NIN
VMEM = 62 * 2**20


def wrap(z):
    return lax.rem(z + NZ, NZ)


def pair_of(z, step):
    odd = lax.rem(z + step, 2)
    return lax.div(wrap(z - step + 2 * step * odd), 2)


def power(exps):
    return lax.shift_left(jnp.int32(1), exps + 3).astype(F32) * 0.125


def rcopy(src, dst, send, recv, device):
    return pltpu.make_async_remote_copy(
        src_ref=src, dst_ref=dst, send_sem=send, recv_sem=recv, device_id=device, device_id_type=MESH
    )


def kernel(
    tc_hbm, te_hbm, tid_hbm, qc_hbm, qe_hbm, qid_hbm, pre_hbm,
    cos_hbm, peak_ref,
    tcode, texp, tfac, tid_ref, qcode, qexp, qid_ref, pre_ref, a_all, b_all, tsq, prod, r1, s2, r2, acc, sx, rx, keep,
    mine, parts, meta, metas, tinv, ppart, peaks, cosv,
    in_sem, z_send, z_recv, x_send, x_recv, s1_send, s1_recv, s2_send, s2_recv, n1_send, n1_recv, n2_send, n2_recv,
    s3_send, s3_recv, a_send, a_recv, m_send, m_recv, p_send, p_recv,
):
    r, c = lax.axis_index("row"), lax.axis_index("col")
    xlo, z = lax.div(r, NZ), lax.rem(r, NZ)
    xhi, y, core = lax.div(c, 8), lax.rem(lax.div(c, 2), 4), lax.rem(c, 2)
    up = (xlo * NZ + wrap(z + 1), c)
    down = (xlo * NZ + wrap(z - 1), c)
    xpair = ((1 - xlo) * NZ + z, c)
    xhop = (r, lax.rem(c + 8, 16))
    diag = ((1 - xlo) * NZ + z, lax.rem(c + 8, 16))
    twin = (r, c + 1 - 2 * core)
    home = xhi == xlo

    barrier = pltpu.get_barrier_semaphore()
    for peer in (up, down, xpair, diag):
        pl.semaphore_signal(barrier, inc=1, device_id=peer, device_id_type=MESH)

    def greet(k, _):
        pl.semaphore_signal(barrier, inc=1, device_id=(r, lax.rem(c + k, 16)), device_id_type=MESH)
        return 0

    lax.fori_loop(1, 16, greet, 0)
    is_self = [jnp.logical_and(2 * c + i == r, lax.div(r, 2) == c) for i in range(2)]
    for i in range(2):
        @pl.when(jnp.logical_not(is_self[i]))
        def _():
            pl.semaphore_signal(barrier, inc=1, device_id=(2 * c + i, lax.div(r, 2)), device_id_type=MESH)

    first_in = [
        pltpu.make_async_copy(src, dst, in_sem.at[NIN + i])
        for i, (src, dst) in enumerate(
            [(qc_hbm, qcode), (qe_hbm, qexp), (pre_hbm, pre_ref), (te_hbm, texp), (tid_hbm, tid_ref), (qid_hbm, qid_ref)]
        )
    ]
    for copy in first_in:
        copy.start()

    def t_in(i):
        rows = pl.ds(i * TCH, TCH)
        return pltpu.make_async_copy(tc_hbm.at[rows], tcode.at[rows], in_sem.at[i])

    for i in range(NIN):
        t_in(i).start()

    for copy in first_in[:3]:
        copy.wait()
    mine_at = pl.multiple_of(z * BLK, BLK)
    q_factor = power(qexp[...]).T
    qsq = jnp.zeros((BLK, LANES), F32)
    for j in range(NBLK):
        cols = pl.ds(j * LANES, LANES)
        value = (qcode[:, cols].astype(F32) * q_factor[:, j : j + 1] * pre_ref[j : j + 1, :]).astype(BF16)
        b_all[pl.ds(mine_at, BLK), cols] = value
        qsq += jnp.square(value.astype(F32))

    pl.semaphore_wait(
        barrier, 4 + 15 + 2 - is_self[0].astype(jnp.int32) - is_self[1].astype(jnp.int32)
    )

    def z_rows(block, k):
        return pl.ds(pl.multiple_of(block * BLK + k * CH, CH), CH)

    def z_copy(way, step, k):
        block, to = (wrap(z - step + 1), up) if way == 0 else (wrap(z + step - 1), down)
        rows = b_all.at[z_rows(block, k)]
        return rcopy(rows, rows, z_send.at[way, step, k], z_recv.at[way, step, k], to)

    def z_arrival(way, step, k):
        block = wrap(z - step) if way == 0 else wrap(z + step)
        rows = b_all.at[z_rows(block, k)]
        return rcopy(rows, rows, z_send.at[way, step, k], z_recv.at[way, step, k], up)

    def chunk_of(way, k):
        return k if way == 0 else (k + NCH // 2) % NCH

    for k in range(NCH):
        for way in range(2):
            z_copy(way, 1, chunk_of(way, k)).start()

    def x_copy(i):
        rows = pl.ds(pl.multiple_of(i * XCH, XCH), XCH)
        there = pl.ds(pl.multiple_of(ROWS + i * XCH, XCH), XCH)
        g = lax.div(i, LANES // XCH)
        return rcopy(a_all.at[rows], a_all.at[there], x_send.at[g], x_recv.at[g], xpair)

    def x_group(g):
        rows = pl.ds(pl.multiple_of(g * LANES, LANES), LANES)
        there = pl.ds(pl.multiple_of(ROWS + g * LANES, LANES), LANES)
        return rcopy(a_all.at[rows], a_all.at[there], x_send.at[g], x_recv.at[g], xpair)

    for copy in first_in[3:]:
        copy.wait()
    tfac[...] = power(texp[...]).T

    def scale(i, _):
        t_in(i).wait()
        rows = pl.ds(pl.multiple_of(i * TCH, TCH), TCH)
        factor = tfac[rows, :]
        total = jnp.zeros((TCH, LANES), F32)
        for j in range(NBLK):
            cols = pl.ds(j * LANES, LANES)
            value = tcode[rows, cols].astype(F32) * factor[:, j : j + 1]
            a_all[rows, cols] = value.astype(BF16)
            total += jnp.square(value)
        tsq[rows, :] = total

        @pl.when(i < 2)
        def _():
            for k in range(XLEAD // 2):
                x_copy(i * (XLEAD // 2) + k).start()

        return 0

    lax.fori_loop(0, NIN, scale, 0)

    mine[...] = jnp.zeros_like(mine)
    for g in range(4):
        mine[g : g + 1, :] = jnp.sum(tsq[pl.ds(g * LANES, LANES), :].T, axis=0, keepdims=True)
    wide = jnp.concatenate([qsq, jnp.zeros_like(qsq)], axis=0)
    mine[4:5, :] = jnp.sum(wide.T, axis=0, keepdims=True)

    def to_col(src, dst, send, recv, k):
        return rcopy(src, dst.at[c], send.at[k], recv.at[c], (r, lax.rem(c + k, 16)))

    def from_col(src, dst, send, recv, k):
        who = lax.rem(c + k, 16)
        return rcopy(src, dst.at[who], send.at[k], recv.at[who], (r, who))

    def send_parts(k, _):
        to_col(mine, parts, a_send, a_recv, k).start()
        return 0

    lax.fori_loop(1, 16, send_parts, 0)
    parts[c] = mine[...]

    def meta_copy(i):
        return rcopy(meta, metas.at[lax.rem(r, 2)], m_send.at[i], m_recv.at[lax.rem(r, 2)], (2 * c + i, lax.div(r, 2)))

    def norms():
        def got(k, _):
            from_col(mine, parts, a_send, a_recv, k).wait_recv()
            return 0

        lax.fori_loop(1, 16, got, 0)
        total = parts[0]
        for k in range(1, 16):
            total += parts[k]
        tinv[...] = math.sqrt(P_SIZE) / jnp.sqrt(total + EPS)
        meta[...] = jnp.zeros_like(meta)
        meta[0:1, :] = total[4:5, :]
        meta[1:2, 0:BLK] = qid_ref[...].astype(F32)
        for i in range(2):
            @pl.when(is_self[i])
            def _():
                metas[i] = meta[...]

            @pl.when(jnp.logical_not(is_self[i]))
            def _():
                meta_copy(i).start()

    last = NZ // 2
    late = lax.rem(z, 2) * BLK
    soon = BLK - late

    def whole(lo, hi):
        return pl.ds(lo, hi - lo), pl.ds(0, LANES)

    def half(lo, hi, q0):
        return pl.ds(lo, hi - lo), pl.ds(pl.multiple_of(q0, BLK), BLK)

    def group(g):
        return pl.ds(g, 1), pl.ds(0, LANES)

    def pair_at(step):
        j = pair_of(z, step)
        return lax.div(j, 2), lax.rem(j, 2)

    def s1_copy(yd, part, i):
        w, q = part
        return rcopy(
            prod.at[yd, 1 - core, w, q], r1.at[yd, w, q], s1_send.at[yd, i], s1_recv.at[yd, i], twin
        )

    def s2_copy(yd, part, i):
        w, q = part
        k = lax.rem(y - yd + 4, 4) - 1
        return rcopy(
            s2.at[yd, w, q], r2.at[k, w, q], s2_send.at[yd, i], s2_recv.at[k, i], (r, xhi * 8 + yd * 2 + core)
        )

    def s2_arrival(k, part, i):
        w, q = part
        return rcopy(r2.at[k, w, q], r2.at[k, w, q], s2_send.at[0, i], s2_recv.at[k, i], twin)

    def dot(step, part):
        w, q = part
        yd, cd = pair_at(step)
        queries = pl.ds(pl.multiple_of((2 * yd + cd) * LANES + q.start, BLK), q.size)
        rows = pl.ds(pl.multiple_of(w.start * LANES, LANES), w.size * LANES)
        value = lax.dot_general(
            b_all[queries, :], a_all[rows, :], (((1,), (1,)), ((), ())), preferred_element_type=F32
        )
        for n in range(w.size):
            prod[yd, cd, w.start + n, q, :] = value[:, n * LANES : (n + 1) * LANES]

    def work(step, part, i):
        yd, cd = pair_at(step)
        dot(step, part)

        @pl.when(core != cd)
        def _():
            s1_copy(yd, part, i).start()

    def relay(step, part, i):
        w, q = part
        yd, cd = pair_at(step)

        @pl.when(core == cd)
        def _():
            s1_copy(yd, part, i).wait_recv()

            @pl.when(y == yd)
            def _():
                acc[w, q, :] = prod[yd, cd, w, q, :] + r1[yd, w, q, :]

            @pl.when(y != yd)
            def _():
                s2[yd, w, q, :] = (prod[yd, cd, w, q, :] + r1[yd, w, q, :]).astype(BF16)
                s2_copy(yd, part, i).start()

    def old(step, what):
        def one(g, _):
            what(step, group(4 + g), 2 + g)
            return 0

        lax.fori_loop(0, lax.div(step - 1, 2), one, 0)

    def new(step, what):
        @pl.when(jnp.logical_and(lax.rem(step, 2) == 0, step > 0))
        def _():
            g = lax.div(step, 2) - 1
            if what is work:
                x_group(g).wait_recv()

            def each(t, _):
                what(t, group(4 + g), 2 + g)
                return 0

            lax.fori_loop(1, step + 1, each, 0)

    def newest_copy():
        return rcopy(prod.at[:, 1 - core, 7], r1.at[:, 7], n1_send, n1_recv, twin)

    def newest_on(n):
        yd = lax.rem(y + n, 4)
        return rcopy(
            s2.at[yd, 7], r2.at[3 - n, 7], n2_send.at[n - 1], n2_recv.at[3 - n], (r, xhi * 8 + yd * 2 + core)
        )

    def work_newest():
        x_group(3).wait_recv()
        value = lax.dot_general(
            b_all[...], a_all[pl.ds(7 * LANES, LANES), :], (((1,), (1,)), ((), ())), preferred_element_type=F32
        )
        for j in range(8):
            prod[j // 2, j % 2, 7] = value[j * LANES : (j + 1) * LANES, :]
        newest_copy().start()

    def relay_newest():
        newest_copy().wait_recv()
        for n in (1, 2, 3):
            yd = lax.rem(y + n, 4)
            s2[yd, 7] = (prod[yd, core, 7] + r1[yd, 7]).astype(BF16)
            newest_on(n).start()
        acc[7] = prod[y, core, 7] + r1[y, 7]

    def arrive(step, k):
        for way in range(2):
            chunk = chunk_of(way, k)

            @pl.when(jnp.logical_or(step < NZ // 2, k < NCH // 2))
            def _():
                z_arrival(way, step, chunk).wait_recv()

            @pl.when(jnp.logical_or(step < NZ // 2 - 1, jnp.logical_and(step == NZ // 2 - 1, k < NCH // 2)))
            def _():
                z_copy(way, step + 1, chunk).start()

    def follow(step, k):
        i = (step - 1) * NCH + k + XLEAD

        @pl.when(i < NX)
        def _():
            x_copy(i).start()

    own = whole(0, 4)

    def body(step, _):
        arrive(step, 0)
        follow(step, 0)

        @pl.when(step > 1)
        def _():
            old(step - 1, work)
            relay(step - 1, own, 0)

        arrive(step, 1)
        follow(step, 1)
        new(step - 1, work)
        arrive(step, 2)
        follow(step, 2)

        @pl.when(step > 1)
        def _():
            old(step - 1, relay)

        new(step - 1, relay)

        @pl.when(step == 2)
        def _():
            norms()

        arrive(step, 3)
        follow(step, 3)
        work(step, own, 0)
        return 0

    lax.fori_loop(1, last, body, 0)
    arrive(last, 0)
    old(last - 1, work)
    relay(last - 1, own, 0)
    work(last, half(0, 4, soon), 0)
    arrive(last, 1)
    work(last, half(0, 4, late), 1)
    old(last - 1, relay)
    relay(last, half(0, 4, soon), 0)
    work(last, half(4, 7, soon), 2)
    relay(last, half(0, 4, late), 1)
    work(last, half(4, 7, late), 3)
    work_newest()
    relay(last, half(4, 7, soon), 2)
    relay(last, half(4, 7, late), 3)
    relay_newest()

    lyd, lcd = pair_at(last)
    is_last = jnp.logical_and(y == lyd, core == lcd)

    def y_arrived(parts_last, parts_else):
        @pl.when(is_last)
        def _():
            for k in range(3):
                for part, i in parts_last:
                    s2_arrival(k, part, i).wait_recv()

        @pl.when(jnp.logical_not(is_last))
        def _():
            for k in range(3):
                for part, i in parts_else:
                    s2_arrival(k, part, i).wait_recv()

    def summed(w):
        return acc[w] + r2[0, w].astype(F32) + r2[1, w].astype(F32) + r2[2, w].astype(F32)

    def s3_own(u):
        return rcopy(sx.at[u], rx.at[0, u], s3_send.at[u], s3_recv.at[0, u], xhop)

    def s3_pair(u):
        return rcopy(sx.at[4 + u], rx.at[0, u], s3_send.at[4 + u], s3_recv.at[0, u], xpair)

    def s3_diag(u):
        return rcopy(sx.at[4 + u], rx.at[1, u], s3_send.at[4 + u], s3_recv.at[1, u], diag)

    own_parts = ([(half(0, 4, soon), 0), (half(0, 4, late), 1)], [(own, 0)])
    old_parts = ([(half(4, 7, soon), 2), (half(4, 7, late), 3)], [(group(4 + g), 2 + g) for g in range(3)])
    y_arrived(*own_parts)
    for u in range(4):
        total = summed(u)

        @pl.when(home)
        def _():
            keep[u] = total

        @pl.when(jnp.logical_not(home))
        def _():
            sx[u] = total.astype(BF16)
            s3_own(u).start()

    for u in range(4):
        if u == 0:
            y_arrived(*old_parts)
        if u == 3:
            for n in (1, 2, 3):
                newest_on(n).wait_recv()
        sx[4 + u] = summed(4 + u).astype(BF16)

        @pl.when(home)
        def _():
            s3_pair(u).start()

        @pl.when(jnp.logical_not(home))
        def _():
            s3_diag(u).start()

    for i in range(2):
        @pl.when(jnp.logical_not(is_self[i]))
        def _():
            rcopy(meta, metas.at[i], m_send.at[i], m_recv.at[i], up).wait_recv()

    lane = lax.broadcasted_iota(jnp.int32, (8, LANES), 1)
    both = jnp.where(lane < BLK, metas[0], pltpu.roll(metas[1], BLK, 1))
    q_inv = jnp.broadcast_to(1.0 / jnp.sqrt(both[0:1, :] + EPS), (LANES, LANES)).T
    q_ids = jnp.broadcast_to(both[1:2, :], (LANES, LANES)).T
    t_ids = tid_ref[...].astype(F32)

    def out_copy(u):
        rows = pl.ds(u * LANES, LANES)
        return pltpu.make_async_copy(cosv.at[rows], cos_hbm.at[rows], in_sem.at[u])

    ppart[...] = jnp.zeros_like(ppart)
    for u in range(4):
        s3_pair(u).wait_recv()

        @pl.when(jnp.logical_not(home))
        def _():
            s3_diag(u).wait_recv()
            keep[u] = rx[1, u].astype(F32)

        raw = keep[u] + rx[0, u].astype(F32)
        value = raw * q_inv * tinv[u : u + 1, :]
        value = jnp.where(q_ids == t_ids[u : u + 1, :], 0.0, value)
        ppart[u : u + 1, :] = jnp.max(value, axis=0, keepdims=True)
        cosv[pl.ds(u * LANES, LANES), :] = value.T

    def send_peaks(k, _):
        to_col(ppart, peaks, p_send, p_recv, k).start()
        return 0

    lax.fori_loop(1, 16, send_peaks, 0)
    peaks[c] = ppart[...]
    for u in range(4):
        out_copy(u).start()

    def sent(step, _):
        for k in range(NCH):
            for way in range(2):
                z_copy(way, step, k).wait_send()
        return 0

    lax.fori_loop(1, NZ // 2, sent, 0)
    for k in range(NCH // 2):
        for way in range(2):
            z_copy(way, NZ // 2, chunk_of(way, k)).wait_send()

    def x_sent(i, _):
        x_group(i).wait_send()
        return 0

    lax.fori_loop(0, 4, x_sent, 0)

    def s_sent(yd, _):
        def out(copy, j):
            for of_last, some in ((True, own_parts[0] + old_parts[0]), (False, own_parts[1] + old_parts[1])):
                @pl.when((j == pair_of(z, last)) == of_last)
                def _():
                    for part, i in some:
                        copy(yd, part, i).wait_send()

        out(s1_copy, 2 * yd + 1 - core)

        @pl.when(yd != y)
        def _():
            out(s2_copy, 2 * yd + core)

        return 0

    lax.fori_loop(0, 4, s_sent, 0)
    newest_copy().wait_send()
    for n in (1, 2, 3):
        newest_on(n).wait_send()
    for u in range(4):
        @pl.when(jnp.logical_not(home))
        def _():
            s3_own(u).wait_send()

        s3_pair(u).wait_send()

    for i in range(2):
        @pl.when(jnp.logical_not(is_self[i]))
        def _():
            meta_copy(i).wait_send()

    def col_done(k, _):
        to_col(mine, parts, a_send, a_recv, k).wait_send()
        to_col(ppart, peaks, p_send, p_recv, k).wait_send()
        from_col(ppart, peaks, p_send, p_recv, k).wait_recv()
        return 0

    lax.fori_loop(1, 16, col_done, 0)
    best = peaks[0]
    for k in range(1, 16):
        best = jnp.maximum(best, peaks[k])
    peak_ref[...] = best[0:4, :]
    for u in range(4):
        out_copy(u).wait()


def shards(train_codes, train_exps, train_ids, query_codes, query_exps, query_ids, precond):
    dma = pltpu.SemaphoreType.DMA
    vmem = pl.BlockSpec(memory_space=pltpu.VMEM)
    hbm = pl.BlockSpec(memory_space=pl.ANY)
    cosines, peak = pl.pallas_call(
        kernel,
        out_shape=(jax.ShapeDtypeStruct((ROWS, LANES), F32), jax.ShapeDtypeStruct((4, LANES), F32)),
        in_specs=[hbm] * 7,
        out_specs=(hbm, vmem),
        scratch_shapes=[
            pltpu.VMEM((ROWS, KD), BF16),
            pltpu.VMEM((NBLK, ROWS), jnp.int32),
            pltpu.VMEM((ROWS, NBLK), F32),
            pltpu.VMEM((4, LANES), jnp.int32),
            pltpu.VMEM((BLK, KD), BF16),
            pltpu.VMEM((NBLK, BLK), jnp.int32),
            pltpu.VMEM((1, BLK), jnp.int32),
            pltpu.VMEM((NBLK, LANES), F32),
            pltpu.VMEM((2 * ROWS, KD), BF16),
            pltpu.VMEM((NZ * BLK, KD), BF16),
            pltpu.VMEM((ROWS, LANES), F32),
            pltpu.VMEM((4, 2, 8, LANES, LANES), F32),
            pltpu.VMEM((4, 8, LANES, LANES), F32),
            pltpu.VMEM((4, 8, LANES, LANES), BF16),
            pltpu.VMEM((3, 8, LANES, LANES), BF16),
            pltpu.VMEM((8, LANES, LANES), F32),
            pltpu.VMEM((8, LANES, LANES), BF16),
            pltpu.VMEM((2, 4, LANES, LANES), BF16),
            pltpu.VMEM((4, LANES, LANES), F32),
            pltpu.VMEM((8, LANES), F32),
            pltpu.VMEM((16, 8, LANES), F32),
            pltpu.VMEM((8, LANES), F32),
            pltpu.VMEM((2, 8, LANES), F32),
            pltpu.VMEM((8, LANES), F32),
            pltpu.VMEM((8, LANES), F32),
            pltpu.VMEM((16, 8, LANES), F32),
            pltpu.VMEM((ROWS, LANES), F32),
            dma((NIN + 6,)),
            dma((2, NZ // 2 + 1, NCH)), dma((2, NZ // 2 + 1, NCH)),
            dma((4,)), dma((4,)),
            dma((4, 5)), dma((4, 5)),
            dma((4, 5)), dma((3, 5)),
            dma, dma, dma((3,)), dma((3,)),
            dma((8,)), dma((2, 4)),
            dma((16,)), dma((16,)),
            dma((2,)), dma((2,)),
            dma((16,)), dma((16,)),
        ],
        compiler_params=pltpu.CompilerParams(
            collective_id=0, has_side_effects=True, vmem_limit_bytes=VMEM
        ),
        cost_estimate=pl.CostEstimate(
            flops=2 * ROWS * 2048 * KD, bytes_accessed=3 * 2**20, transcendentals=0
        ),
    )(
        train_codes, train_exps.T, train_ids.reshape(4, LANES), query_codes, query_exps.T,
        query_ids.reshape(1, BLK), precond.reshape(NBLK, LANES),
    )
    return cosines, peak.reshape(ROWS)


def solution(mesh):
    in_specs = (
        P("row", "col"),
        P("row", "col"),
        P("row"),
        P("row", "col"),
        P("row", "col"),
        P("row"),
        P("col"),
    )
    out_specs = (P("row", "col"), P("row"))
    return jax.shard_map(shards, mesh=mesh, in_specs=in_specs, out_specs=out_specs, check_vma=False)
```

```python
import functools
import math

import jax
import jax.numpy as jnp
from jax import lax
from jax.experimental import pallas as pl
from jax.experimental.pallas import tpu as pltpu
from jax.sharding import PartitionSpec as P

P_SIZE = 32768
EPS = 1e-06
MESH = pl.DeviceIdType.MESH
F32 = jnp.float32
BF16 = jnp.bfloat16

NZ = 16
BLK = 64
KD = 2048
ROWS = 512
LANES = 128
NBLK = KD // LANES
NCH = 2
CH = BLK // NCH
XCH = 16
NX = ROWS // XCH
XLEAD = 4
NIN = 8
TCH = ROWS // NIN
VMEM = 62 * 2**20


def wrap(z):
    return lax.rem(z + NZ, NZ)


def pair_of(z, step):
    odd = lax.rem(z + step, 2)
    return lax.div(wrap(z - step + 2 * step * odd), 2)


def power(exps):
    return lax.shift_left(jnp.int32(1), exps + 3).astype(F32) * 0.125


def rcopy(src, dst, send, recv, device):
    return pltpu.make_async_remote_copy(
        src_ref=src, dst_ref=dst, send_sem=send, recv_sem=recv, device_id=device, device_id_type=MESH
    )


def kernel(
    tc_hbm, te_hbm, tid_hbm, qc_hbm, qe_hbm, qid_hbm, pre_hbm,
    cos_ref, peaks,
    tcode, texp, tfac, tid_ref, qcode, qexp, qid_ref, pre_ref, a_all, b_all, tsq, prod, r1, s2, r2, acc, sx, rx, keep,
    mine, parts, meta, metas, tinv, ppart,
    in_sem, z_send, z_recv, x_send, x_recv, s1_send, s1_recv, s2_send, s2_recv, n1_send, n1_recv, n2_send, n2_recv,
    s3_send, s3_recv, a_send, a_recv, m_send, m_recv, p_send, p_recv,
):
    r, c = lax.axis_index("row"), lax.axis_index("col")
    xlo, z = lax.div(r, NZ), lax.rem(r, NZ)
    xhi, y, core = lax.div(c, 8), lax.rem(lax.div(c, 2), 4), lax.rem(c, 2)
    up = (xlo * NZ + wrap(z + 1), c)
    down = (xlo * NZ + wrap(z - 1), c)
    xpair = ((1 - xlo) * NZ + z, c)
    xhop = (r, lax.rem(c + 8, 16))
    diag = ((1 - xlo) * NZ + z, lax.rem(c + 8, 16))
    twin = (r, c + 1 - 2 * core)
    home = xhi == xlo

    first_in = [
        pltpu.make_async_copy(src, dst, in_sem.at[NIN + i])
        for i, (src, dst) in enumerate(
            [(qc_hbm, qcode), (qe_hbm, qexp), (pre_hbm, pre_ref), (te_hbm, texp), (tid_hbm, tid_ref), (qid_hbm, qid_ref)]
        )
    ]
    for copy in first_in[:3]:
        copy.start()

    barrier = pltpu.get_barrier_semaphore()
    for peer in (up, down, xpair, diag):
        pl.semaphore_signal(barrier, inc=1, device_id=peer, device_id_type=MESH)

    def greet(k, _):
        pl.semaphore_signal(barrier, inc=1, device_id=(r, lax.rem(c + k, 16)), device_id_type=MESH)
        return 0

    lax.fori_loop(1, 16, greet, 0)
    is_self = [jnp.logical_and(2 * c + i == r, lax.div(r, 2) == c) for i in range(2)]
    for i in range(2):
        @pl.when(jnp.logical_not(is_self[i]))
        def _():
            pl.semaphore_signal(barrier, inc=1, device_id=(2 * c + i, lax.div(r, 2)), device_id_type=MESH)

    for copy in first_in[3:]:
        copy.start()

    def t_in(i):
        rows = pl.ds(i * TCH, TCH)
        return pltpu.make_async_copy(tc_hbm.at[rows], tcode.at[rows], in_sem.at[i])

    for i in range(NIN):
        t_in(i).start()

    for copy in first_in[:3]:
        copy.wait()
    mine_at = pl.multiple_of(z * BLK, BLK)
    q_factor = power(qexp[...]).T
    qsq = jnp.zeros((BLK, LANES), F32)
    for j in range(NBLK):
        cols = pl.ds(j * LANES, LANES)
        value = (qcode[:, cols].astype(F32) * q_factor[:, j : j + 1] * pre_ref[j : j + 1, :]).astype(BF16)
        b_all[pl.ds(mine_at, BLK), cols] = value
        qsq += jnp.square(value.astype(F32))

    pl.semaphore_wait(
        barrier, 4 + 15 + 2 - is_self[0].astype(jnp.int32) - is_self[1].astype(jnp.int32)
    )

    def z_rows(block, k):
        return pl.ds(pl.multiple_of(block * BLK + k * CH, CH), CH)

    def z_copy(way, step, k):
        block, to = (wrap(z - step + 1), up) if way == 0 else (wrap(z + step - 1), down)
        rows = b_all.at[z_rows(block, k)]
        return rcopy(rows, rows, z_send.at[way, step], z_recv.at[way, step, k], to)

    def z_arrival(way, step, k):
        block = wrap(z - step) if way == 0 else wrap(z + step)
        rows = b_all.at[z_rows(block, k)]
        return rcopy(rows, rows, z_send.at[way, step], z_recv.at[way, step, k], up)

    def z_left(step, rows):
        for way in range(2):
            whole_block = b_all.at[pl.ds(0, rows)]
            rcopy(whole_block, whole_block, z_send.at[way, step], z_recv.at[way, step, 0], up).wait_send()

    def chunk_of(way, k):
        return k if way == 0 else (k + NCH // 2) % NCH

    for k in range(NCH):
        for way in range(2):
            z_copy(way, 1, chunk_of(way, k)).start()

    def x_copy(i):
        rows = pl.ds(pl.multiple_of(i * XCH, XCH), XCH)
        there = pl.ds(pl.multiple_of(ROWS + i * XCH, XCH), XCH)
        g = lax.div(i, LANES // XCH)
        return rcopy(a_all.at[rows], a_all.at[there], x_send.at[g], x_recv.at[g], xpair)

    def x_group(g):
        rows = pl.ds(pl.multiple_of(g * LANES, LANES), LANES)
        there = pl.ds(pl.multiple_of(ROWS + g * LANES, LANES), LANES)
        return rcopy(a_all.at[rows], a_all.at[there], x_send.at[g], x_recv.at[g], xpair)

    for copy in first_in[3:]:
        copy.wait()
    tfac[...] = power(texp[...]).T

    def scale(i, _):
        t_in(i).wait()
        rows = pl.ds(pl.multiple_of(i * TCH, TCH), TCH)
        factor = tfac[rows, :]
        total = jnp.zeros((TCH, LANES), F32)
        for j in range(NBLK):
            cols = pl.ds(j * LANES, LANES)
            value = tcode[rows, cols].astype(F32) * factor[:, j : j + 1]
            a_all[rows, cols] = value.astype(BF16)
            total += jnp.square(value)
        tsq[rows, :] = total

        @pl.when(i < 2)
        def _():
            for k in range(XLEAD // 2):
                x_copy(i * (XLEAD // 2) + k).start()

        return 0

    lax.fori_loop(0, NIN, scale, 0)

    mine[...] = jnp.zeros_like(mine)
    for g in range(4):
        mine[g : g + 1, :] = jnp.sum(tsq[pl.ds(g * LANES, LANES), :].T, axis=0, keepdims=True)
    wide = jnp.concatenate([qsq, jnp.zeros_like(qsq)], axis=0)
    mine[4:5, :] = jnp.sum(wide.T, axis=0, keepdims=True)

    def to_col(src, dst, send, recv, k):
        return rcopy(src, dst.at[c], send, recv, (r, lax.rem(c + k, 16)))

    def all_of_col(dst, send, recv):
        fifteen = dst.at[pl.ds(0, 15)]
        return rcopy(fifteen, fifteen, send, recv, twin)

    def send_parts(k, _):
        to_col(mine, parts, a_send, a_recv, k).start()
        return 0

    lax.fori_loop(1, 16, send_parts, 0)
    parts[c] = mine[...]

    def meta_copy(i):
        return rcopy(meta, metas.at[lax.rem(r, 2)], m_send.at[i], m_recv.at[lax.rem(r, 2)], (2 * c + i, lax.div(r, 2)))

    def norms():
        all_of_col(parts, a_send, a_recv).wait()
        total = parts[0]
        for k in range(1, 16):
            total += parts[k]
        tinv[...] = math.sqrt(P_SIZE) / jnp.sqrt(total + EPS)
        meta[...] = jnp.zeros_like(meta)
        meta[0:1, :] = total[4:5, :]
        meta[1:2, 0:BLK] = qid_ref[...].astype(F32)
        for i in range(2):
            @pl.when(is_self[i])
            def _():
                metas[i] = meta[...]

            @pl.when(jnp.logical_not(is_self[i]))
            def _():
                meta_copy(i).start()

    last = NZ // 2
    late = lax.rem(z, 2) * BLK
    soon = BLK - late

    def whole(lo, hi):
        return pl.ds(lo, hi - lo), pl.ds(0, LANES)

    def half(lo, hi, q0):
        return pl.ds(lo, hi - lo), pl.ds(pl.multiple_of(q0, BLK), BLK)

    def group(g):
        return pl.ds(g, 1), pl.ds(0, LANES)

    def pair_at(step):
        j = pair_of(z, step)
        return lax.div(j, 2), lax.rem(j, 2)

    def s1_copy(yd, part, i):
        w, q = part
        return rcopy(
            prod.at[yd, 1 - core, w, q], r1.at[yd, w, q], s1_send.at[yd, i], s1_recv.at[yd, i], twin
        )

    def s2_copy(yd, part, i):
        w, q = part
        k = lax.rem(y - yd + 4, 4) - 1
        return rcopy(
            s2.at[yd, w, q], r2.at[k, w, q], s2_send.at[yd, i], s2_recv.at[i], (r, xhi * 8 + yd * 2 + core)
        )

    def s2_arrival(part, i):
        w, q = part
        return rcopy(r2.at[:, w, q], r2.at[:, w, q], s2_send.at[0, i], s2_recv.at[i], twin)

    def dot(step, part):
        w, q = part
        yd, cd = pair_at(step)
        queries = pl.ds(pl.multiple_of((2 * yd + cd) * LANES + q.start, BLK), q.size)
        rows = pl.ds(pl.multiple_of(w.start * LANES, LANES), w.size * LANES)
        value = lax.dot_general(
            b_all[queries, :], a_all[rows, :], (((1,), (1,)), ((), ())), preferred_element_type=F32
        )
        for n in range(w.size):
            prod[yd, cd, w.start + n, q, :] = value[:, n * LANES : (n + 1) * LANES]

    def work(step, part, i):
        yd, cd = pair_at(step)
        dot(step, part)

        @pl.when(core != cd)
        def _():
            s1_copy(yd, part, i).start()

    def relay(step, part, i):
        w, q = part
        yd, cd = pair_at(step)

        @pl.when(core == cd)
        def _():
            s1_copy(yd, part, i).wait_recv()

            @pl.when(y == yd)
            def _():
                acc[w, q, :] = prod[yd, cd, w, q, :] + r1[yd, w, q, :]

            @pl.when(y != yd)
            def _():
                s2[yd, w, q, :] = (prod[yd, cd, w, q, :] + r1[yd, w, q, :]).astype(BF16)
                s2_copy(yd, part, i).start()

    def old(step, what):
        def one(g, _):
            what(step, group(4 + g), 2 + g)
            return 0

        lax.fori_loop(0, lax.div(step - 1, 2), one, 0)

    def new(step, what):
        @pl.when(jnp.logical_and(lax.rem(step, 2) == 0, step > 0))
        def _():
            g = lax.div(step, 2) - 1
            if what is work:
                x_group(g).wait_recv()

            def each(t, _):
                what(t, group(4 + g), 2 + g)
                return 0

            lax.fori_loop(1, step + 1, each, 0)

    def newest_copy():
        return rcopy(prod.at[:, 1 - core, 7], r1.at[:, 7], n1_send, n1_recv, twin)

    def newest_on(n):
        yd = lax.rem(y + n, 4)
        return rcopy(
            s2.at[yd, 7], r2.at[3 - n, 7], n2_send, n2_recv, (r, xhi * 8 + yd * 2 + core)
        )

    def newest_all():
        return rcopy(r2.at[:, 7], r2.at[:, 7], n2_send, n2_recv, twin)

    def work_newest():
        x_group(3).wait_recv()
        value = lax.dot_general(
            b_all[...], a_all[pl.ds(7 * LANES, LANES), :], (((1,), (1,)), ((), ())), preferred_element_type=F32
        )
        for j in range(8):
            prod[j // 2, j % 2, 7] = value[j * LANES : (j + 1) * LANES, :]
        newest_copy().start()

    def relay_newest():
        newest_copy().wait_recv()
        for n in (1, 2, 3):
            yd = lax.rem(y + n, 4)
            s2[yd, 7] = (prod[yd, core, 7] + r1[yd, 7]).astype(BF16)
            newest_on(n).start()
        acc[7] = prod[y, core, 7] + r1[y, 7]

    def arrive(step, slot):
        if slot % (4 // NCH):
            return
        k = slot // (4 // NCH)
        for way in range(2):
            chunk = chunk_of(way, k)

            @pl.when(jnp.logical_or(step < NZ // 2, k < NCH // 2))
            def _():
                z_arrival(way, step, chunk).wait_recv()

            @pl.when(jnp.logical_or(step < NZ // 2 - 1, jnp.logical_and(step == NZ // 2 - 1, k < NCH // 2)))
            def _():
                z_copy(way, step + 1, chunk).start()

    def follow(step, k):
        i = (step - 1) * 4 + k + XLEAD

        @pl.when(i < NX)
        def _():
            x_copy(i).start()

    own = whole(0, 4)
    most = whole(0, 7)
    first = half(0, 7, soon)
    ends = (half(0, 4, late), half(4, 7, late))

    def body(step, _):
        arrive(step, 0)
        follow(step, 0)

        @pl.when(step > 1)
        def _():
            old(step - 1, work)
            relay(step - 1, own, 0)

        arrive(step, 1)
        follow(step, 1)
        new(step - 1, work)
        arrive(step, 2)
        follow(step, 2)

        @pl.when(step > 1)
        def _():
            old(step - 1, relay)
            z_left(step - 1, BLK)

        new(step - 1, relay)

        @pl.when(step == 2)
        def _():
            norms()

        arrive(step, 3)
        follow(step, 3)

        @pl.when(step < last - 1)
        def _():
            work(step, own, 0)

        return 0

    lax.fori_loop(1, last, body, 0)

    yd7, cd7 = pair_at(last - 1)
    yd8, cd8 = pair_at(last)
    at7 = pl.ds(pl.multiple_of((2 * yd7 + cd7) * LANES, LANES), LANES)
    at8 = pl.ds(pl.multiple_of((2 * yd8 + cd8) * LANES + soon, BLK), BLK)
    value = lax.dot_general(
        jnp.concatenate([b_all[at7, :], b_all[at8, :]], axis=0), a_all[pl.ds(0, 7 * LANES), :],
        (((1,), (1,)), ((), ())), preferred_element_type=F32,
    )
    for n in range(7):
        prod[yd7, cd7, n] = value[:LANES, n * LANES : (n + 1) * LANES]
        prod[yd8, cd8, n, first[1], :] = value[LANES:, n * LANES : (n + 1) * LANES]
    for step, part in ((last - 1, most), (last, first)):
        @pl.when(core != pair_at(step)[1])
        def _():
            s1_copy(pair_at(step)[0], part, 0).start()

    arrive(last, 0)
    relay(last - 1, most, 0)
    relay(last, first, 0)
    arrive(last, 1)
    work(last, ends[0], 1)
    work(last, ends[1], 2)
    relay(last, ends[0], 1)
    relay(last, ends[1], 2)
    work_newest()
    relay_newest()

    j_last, j_before = pair_of(z, last), pair_of(z, last - 1)
    of_own = ([(first, 0), (ends[0], 1)], [(most, 0)], [(own, 0)])
    of_old = ([(ends[1], 2)], [], [(group(4 + g), 2 + g) for g in range(3)])

    def by_pair(j, cases, do):
        is_one, is_two = j == j_last, j == j_before
        tests = (is_one, is_two, jnp.logical_not(jnp.logical_or(is_one, is_two)))
        for test, some in zip(tests, cases):
            if some:
                @pl.when(test)
                def _():
                    for part, i in some:
                        do(part, i)

    def y_arrived(cases):
        by_pair(2 * y + core, cases, lambda part, i: s2_arrival(part, i).wait_recv())

    def summed(w):
        return acc[w] + r2[0, w].astype(F32) + r2[1, w].astype(F32) + r2[2, w].astype(F32)

    def s3_own(u):
        return rcopy(sx.at[u], rx.at[0, u], s3_send.at[u], s3_recv.at[0, u], xhop)

    def s3_pair(u):
        return rcopy(sx.at[4 + u], rx.at[0, u], s3_send.at[4 + u], s3_recv.at[0, u], xpair)

    def s3_diag(u):
        return rcopy(sx.at[4 + u], rx.at[1, u], s3_send.at[4 + u], s3_recv.at[1, u], diag)

    y_arrived(of_own)
    for u in range(4):
        total = summed(u)

        @pl.when(home)
        def _():
            keep[u] = total

        @pl.when(jnp.logical_not(home))
        def _():
            sx[u] = total.astype(BF16)
            s3_own(u).start()

    for u in range(4):
        if u == 0:
            y_arrived(of_old)
        if u == 3:
            newest_all().wait_recv()
        sx[4 + u] = summed(4 + u).astype(BF16)

        @pl.when(home)
        def _():
            s3_pair(u).start()

        @pl.when(jnp.logical_not(home))
        def _():
            s3_diag(u).start()

    def left(yd, _):
        def out(copy, j):
            by_pair(j, [a + b for a, b in zip(of_own, of_old)], lambda part, i: copy(yd, part, i).wait_send())

        out(s1_copy, 2 * yd + 1 - core)

        @pl.when(yd != y)
        def _():
            out(s2_copy, 2 * yd + core)

        return 0

    lax.fori_loop(0, 4, left, 0)
    z_left(last - 1, BLK)
    z_left(last, BLK // 2)
    for g in range(4):
        x_group(g).wait_send()
    newest_copy().wait_send()
    newest_all().wait_send()
    for i in range(2):
        @pl.when(jnp.logical_not(is_self[i]))
        def _():
            meta_copy(i).wait_send()

    for i in range(2):
        @pl.when(jnp.logical_not(is_self[i]))
        def _():
            rcopy(meta, metas.at[i], m_send.at[i], m_recv.at[i], up).wait_recv()

    lane = lax.broadcasted_iota(jnp.int32, (8, LANES), 1)
    both = jnp.where(lane < BLK, metas[0], pltpu.roll(metas[1], BLK, 1))
    q_inv = jnp.broadcast_to(1.0 / jnp.sqrt(both[0:1, :] + EPS), (LANES, LANES)).T
    q_ids = jnp.broadcast_to(both[1:2, :], (LANES, LANES)).T
    t_ids = tid_ref[...].astype(F32)

    ppart[...] = jnp.zeros_like(ppart)
    for u in range(4):
        s3_pair(u).wait_recv()

        @pl.when(jnp.logical_not(home))
        def _():
            s3_diag(u).wait_recv()
            keep[u] = rx[1, u].astype(F32)

        raw = keep[u] + rx[0, u].astype(F32)
        value = raw * q_inv * tinv[u : u + 1, :]
        value = jnp.where(q_ids == t_ids[u : u + 1, :], 0.0, value)
        ppart[u : u + 1, :] = jnp.max(value, axis=0, keepdims=True)
        cos_ref[u] = value

    def send_peaks(k, _):
        to_col(ppart, peaks, p_send, p_recv, k).start()
        return 0

    lax.fori_loop(1, 16, send_peaks, 0)
    peaks[c] = ppart[...]
    for u in range(4):
        @pl.when(jnp.logical_not(home))
        def _():
            s3_own(u).wait_send()

        s3_pair(u).wait_send()

    all_of_col(peaks, p_send, p_recv).wait()


def lay_out(tiles, peaks, cos_ref, peak_ref):
    for u in range(4):
        cos_ref[pl.ds(u * LANES, LANES), :] = tiles[u].T
    best = peaks[0]
    for k in range(1, 16):
        best = jnp.maximum(best, peaks[k])
    peak_ref[...] = best[0:4, :]


def shards(train_codes, train_exps, train_ids, query_codes, query_exps, query_ids, precond):
    dma = pltpu.SemaphoreType.DMA
    vmem = pl.BlockSpec(memory_space=pltpu.VMEM)
    hbm = pl.BlockSpec(memory_space=pl.ANY)
    tiles, peaks = pl.pallas_call(
        kernel,
        out_shape=(pltpu.VMEM((4, LANES, LANES), F32), pltpu.VMEM((16, 8, LANES), F32)),
        in_specs=[hbm] * 7,
        out_specs=(vmem, vmem),
        scratch_shapes=[
            pltpu.VMEM((ROWS, KD), BF16),
            pltpu.VMEM((NBLK, ROWS), jnp.int32),
            pltpu.VMEM((ROWS, NBLK), F32),
            pltpu.VMEM((4, LANES), jnp.int32),
            pltpu.VMEM((BLK, KD), BF16),
            pltpu.VMEM((NBLK, BLK), jnp.int32),
            pltpu.VMEM((1, BLK), jnp.int32),
            pltpu.VMEM((NBLK, LANES), F32),
            pltpu.VMEM((2 * ROWS, KD), BF16),
            pltpu.VMEM((NZ * BLK, KD), BF16),
            pltpu.VMEM((ROWS, LANES), F32),
            pltpu.VMEM((4, 2, 8, LANES, LANES), F32),
            pltpu.VMEM((4, 8, LANES, LANES), F32),
            pltpu.VMEM((4, 8, LANES, LANES), BF16),
            pltpu.VMEM((3, 8, LANES, LANES), BF16),
            pltpu.VMEM((8, LANES, LANES), F32),
            pltpu.VMEM((8, LANES, LANES), BF16),
            pltpu.VMEM((2, 4, LANES, LANES), BF16),
            pltpu.VMEM((4, LANES, LANES), F32),
            pltpu.VMEM((8, LANES), F32),
            pltpu.VMEM((16, 8, LANES), F32),
            pltpu.VMEM((8, LANES), F32),
            pltpu.VMEM((2, 8, LANES), F32),
            pltpu.VMEM((8, LANES), F32),
            pltpu.VMEM((8, LANES), F32),
            dma((NIN + 6,)),
            dma((2, NZ // 2 + 1)), dma((2, NZ // 2 + 1, NCH)),
            dma((4,)), dma((4,)),
            dma((4, 5)), dma((4, 5)),
            dma((4, 5)), dma((5,)),
            dma, dma, dma, dma,
            dma((8,)), dma((2, 4)),
            dma, dma,
            dma((2,)), dma((2,)),
            dma, dma,
        ],
        compiler_params=pltpu.CompilerParams(
            collective_id=0, has_side_effects=True, vmem_limit_bytes=VMEM
        ),
        cost_estimate=pl.CostEstimate(
            flops=2 * ROWS * 2048 * KD, bytes_accessed=3 * 2**20, transcendentals=0
        ),
    )(
        train_codes, train_exps.T, train_ids.reshape(4, LANES), query_codes, query_exps.T,
        query_ids.reshape(1, BLK), precond.reshape(NBLK, LANES),
    )
    cosines, peak = pl.pallas_call(
        lay_out,
        out_shape=(jax.ShapeDtypeStruct((ROWS, LANES), F32), jax.ShapeDtypeStruct((4, LANES), F32)),
        in_specs=[vmem, vmem],
        out_specs=(vmem, vmem),
    )(tiles, peaks)
    return cosines, peak.reshape(ROWS)


def solution(mesh):
    in_specs = (
        P("row", "col"),
        P("row", "col"),
        P("row"),
        P("row", "col"),
        P("row", "col"),
        P("row"),
        P("col"),
    )
    out_specs = (P("row", "col"), P("row"))
    return jax.shard_map(shards, mesh=mesh, in_specs=in_specs, out_specs=out_specs, check_vma=False)
```

```python
import functools
import math

import jax
import jax.numpy as jnp
from jax import lax
from jax.experimental import pallas as pl
from jax.experimental.pallas import tpu as pltpu
from jax.sharding import PartitionSpec as P

P_SIZE = 32768
EPS = 1e-06
MESH = pl.DeviceIdType.MESH
F32 = jnp.float32
BF16 = jnp.bfloat16

NZ = 16
BLK = 64
KD = 2048
ROWS = 512
LANES = 128
NBLK = KD // LANES
NCH = 4
CH = BLK // NCH
XCH = 16
NX = ROWS // XCH
XLEAD = 4
NIN = 8
TCH = ROWS // NIN
VMEM = 62 * 2**20


def wrap(z):
    return lax.rem(z + NZ, NZ)


def pair_of(z, step):
    odd = lax.rem(z + step, 2)
    return lax.div(wrap(z - step + 2 * step * odd), 2)


def power(exps):
    return lax.shift_left(jnp.int32(1), exps + 3).astype(F32) * 0.125


def rcopy(src, dst, send, recv, device):
    return pltpu.make_async_remote_copy(
        src_ref=src, dst_ref=dst, send_sem=send, recv_sem=recv, device_id=device, device_id_type=MESH
    )


def kernel(
    tc_hbm, te_hbm, tid_hbm, qc_hbm, qe_hbm, qid_hbm, pre_hbm,
    cos_ref, peaks,
    tcode, texp, tfac, tid_ref, qcode, qexp, qid_ref, pre_ref, a_all, b_all, tsq, prod, r1, s2, r2, rf, acc, sx, rx, keep,
    mine, parts, tots, metas, qparts, mtot, mpair, tinv, ppart,
    in_sem, z_send, z_recv, x_send, x_recv, s1_send, s1_recv, s2_send, s2_recv, c_send, c_recv, f_recv, n1_send, n1_recv, n2_send, n2_recv,
    s3_send, s3_recv, t_send, t_recv, m_send, m_recv, mp_send, mp_recv, q_send, q_recv, p_send, p_recv,
):
    r, c = lax.axis_index("row"), lax.axis_index("col")
    xlo, z = lax.div(r, NZ), lax.rem(r, NZ)
    xhi, y, core = lax.div(c, 8), lax.rem(lax.div(c, 2), 4), lax.rem(c, 2)
    up = (xlo * NZ + wrap(z + 1), c)
    down = (xlo * NZ + wrap(z - 1), c)
    xpair = ((1 - xlo) * NZ + z, c)
    xhop = (r, lax.rem(c + 8, 16))
    diag = ((1 - xlo) * NZ + z, lax.rem(c + 8, 16))
    twin = (r, c + 1 - 2 * core)
    home = xhi == xlo

    def y_dev(to):
        return (r, xhi * 8 + lax.rem(to, 4) * 2 + core)


    first_in = [
        pltpu.make_async_copy(src, dst, in_sem.at[NIN + i])
        for i, (src, dst) in enumerate(
            [(qc_hbm, qcode), (qe_hbm, qexp), (pre_hbm, pre_ref), (te_hbm, texp), (tid_hbm, tid_ref), (qid_hbm, qid_ref)]
        )
    ]
    for copy in first_in[:3]:
        copy.start()

    barrier = pltpu.get_barrier_semaphore()
    for peer in (up, down, xpair, diag, xhop, twin, y_dev(y + 1), y_dev(y + 2), y_dev(y + 3)):
        pl.semaphore_signal(barrier, inc=1, device_id=peer, device_id_type=MESH)

    for copy in first_in[3:]:
        copy.start()

    def t_in(i):
        rows = pl.ds(i * TCH, TCH)
        return pltpu.make_async_copy(tc_hbm.at[rows], tcode.at[rows], in_sem.at[i])

    for i in range(NIN):
        t_in(i).start()

    for copy in first_in[:3]:
        copy.wait()
    mine_at = pl.multiple_of(z * BLK, BLK)
    q_factor = power(qexp[...]).T
    qsq = jnp.zeros((BLK, LANES), F32)
    for j in range(NBLK):
        cols = pl.ds(j * LANES, LANES)
        value = (qcode[:, cols].astype(F32) * q_factor[:, j : j + 1] * pre_ref[j : j + 1, :]).astype(BF16)
        b_all[pl.ds(mine_at, BLK), cols] = value
        qsq += jnp.square(value.astype(F32))

    first_in[5].wait()
    wide = jnp.concatenate([qsq, jnp.zeros_like(qsq)], axis=0)
    metas[z] = jnp.zeros((8, LANES), F32)
    metas[z, 0:1, :] = jnp.sum(wide.T, axis=0, keepdims=True)
    metas[z, 1:2, 0:BLK] = qid_ref[...].astype(F32)
    pl.semaphore_wait(barrier, 9)

    def z_rows(block, k):
        return pl.ds(pl.multiple_of(block * BLK + k * CH, CH), CH)

    def z_copy(way, step, k):
        block, to = (wrap(z - step + 1), up) if way == 0 else (wrap(z + step - 1), down)
        rows = b_all.at[z_rows(block, k)]
        return rcopy(rows, rows, z_send.at[way, step], z_recv.at[way, step, k], to)

    def z_arrival(way, step, k):
        block = wrap(z - step) if way == 0 else wrap(z + step)
        rows = b_all.at[z_rows(block, k)]
        return rcopy(rows, rows, z_send.at[way, step], z_recv.at[way, step, k], up)

    def z_left(step, rows):
        for way in range(2):
            whole_block = b_all.at[pl.ds(0, rows)]
            rcopy(whole_block, whole_block, z_send.at[way, step], z_recv.at[way, step, 0], up).wait_send()

    def chunk_of(way, k):
        return k if way == 0 else (k + NCH // 2) % NCH

    def m_copy(way, hop):
        block, to = (wrap(z - hop + 1), up) if way == 0 else (wrap(z + hop - 1), down)
        return rcopy(metas.at[block], metas.at[block], m_send.at[way], m_recv.at[way, hop], to)

    def m_pass(hop):
        for way in range(2):
            block = wrap(z - hop) if way == 0 else wrap(z + hop)

            @pl.when(hop + way <= NZ // 2)
            def _():
                rcopy(metas.at[block], metas.at[block], m_send.at[way], m_recv.at[way, hop], up).wait_recv()

            @pl.when(hop + way < NZ // 2)
            def _():
                m_copy(way, hop + 1).start()

    for k in range(NCH):
        for way in range(2):
            z_copy(way, 1, chunk_of(way, k)).start()
            if k == 1:
                m_copy(way, 1).start()

    def x_copy(i):
        rows = pl.ds(pl.multiple_of(i * XCH, XCH), XCH)
        there = pl.ds(pl.multiple_of(ROWS + i * XCH, XCH), XCH)
        g = lax.div(i, LANES // XCH)
        return rcopy(a_all.at[rows], a_all.at[there], x_send.at[g], x_recv.at[g], xpair)

    def x_group(g):
        rows = pl.ds(pl.multiple_of(g * LANES, LANES), LANES)
        there = pl.ds(pl.multiple_of(ROWS + g * LANES, LANES), LANES)
        return rcopy(a_all.at[rows], a_all.at[there], x_send.at[g], x_recv.at[g], xpair)

    for copy in first_in[3:5]:
        copy.wait()
    tfac[...] = power(texp[...]).T

    def scale(i, _):
        t_in(i).wait()
        rows = pl.ds(pl.multiple_of(i * TCH, TCH), TCH)
        factor = tfac[rows, :]
        total = jnp.zeros((TCH, LANES), F32)
        for j in range(NBLK):
            cols = pl.ds(j * LANES, LANES)
            value = tcode[rows, cols].astype(F32) * factor[:, j : j + 1]
            a_all[rows, cols] = value.astype(BF16)
            total += jnp.square(value)
        tsq[rows, :] = total

        @pl.when(i < 2)
        def _():
            for k in range(XLEAD // 2):
                x_copy(i * (XLEAD // 2) + k).start()

        return 0

    lax.fori_loop(0, NIN, scale, 0)

    mine[...] = jnp.zeros_like(mine)
    for g in range(4):
        mine[g : g + 1, :] = jnp.sum(tsq[pl.ds(g * LANES, LANES), :].T, axis=0, keepdims=True)

    def to_col(src, dst, send, recv, k):
        return rcopy(src, dst.at[c], send, recv, (r, lax.rem(c + k, 16)))

    def all_of_col(dst, send, recv):
        fifteen = dst.at[pl.ds(0, 15)]
        return rcopy(fifteen, fifteen, send, recv, twin)

    def t_copy(k):
        src, to = (mine, twin) if k == 0 else (tots.at[1], xhop) if k == 4 else (tots.at[0], y_dev(y + k))
        return rcopy(src, parts.at[k], t_send.at[k], t_recv.at[k], to)

    t_copy(0).start()

    def q_copy(n):
        return rcopy(metas.at[pl.ds(2 * n, 2)], qparts.at[c], q_send, q_recv, (r, 8 * xlo + n))

    def q_sent(count):
        some = qparts.at[pl.ds(0, count)]
        return rcopy(some, some, q_send, q_recv, twin)

    def m_pair():
        return rcopy(mtot, mpair, mp_send, mp_recv, xpair)

    def send_shares():
        def one(n, _):
            @pl.when(8 * xlo + n != c)
            def _():
                q_copy(n).start()

            return 0

        lax.fori_loop(0, 8, one, 0)

        @pl.when(home)
        def _():
            qparts[c] = metas[pl.ds(4 * y + 2 * core, 2)]

    def sum_shares():
        @pl.when(home)
        def _():
            q_sent(15).wait_recv()
            total = qparts[0]
            for k in range(1, 16):
                total += qparts[k]
            row = lax.broadcasted_iota(jnp.int32, total.shape, 1)
            mtot[...] = jnp.where(row == 0, total, metas[pl.ds(4 * y + 2 * core, 2)])
            m_pair().start()
            mpair[...] = mtot[...]

    def norms(phase):
        if phase == 1:
            t_copy(0).wait_recv()
            tots[0] = mine[...] + parts[0]
            for k in (1, 2, 3):
                t_copy(k).start()
        elif phase == 2:
            for k in (1, 2, 3):
                t_copy(k).wait_recv()
            tots[1] = tots[0] + parts[1] + parts[2] + parts[3]
            t_copy(4).start()
        else:
            t_copy(4).wait_recv()
            tinv[...] = math.sqrt(P_SIZE) / jnp.sqrt(tots[1] + parts[4] + EPS)

    last = NZ // 2
    late = lax.rem(z, 2) * BLK
    soon = BLK - late

    def whole(lo, hi):
        return pl.ds(lo, hi - lo), pl.ds(0, LANES)

    def half(lo, hi, q0):
        return pl.ds(lo, hi - lo), pl.ds(pl.multiple_of(q0, BLK), BLK)

    def group(g):
        return pl.ds(g, 1), pl.ds(0, LANES)

    def pair_at(step):
        j = pair_of(z, step)
        return lax.div(j, 2), lax.rem(j, 2)

    def s1_copy(yd, part, i):
        w, q = part
        return rcopy(
            prod.at[yd, 1 - core, w, q], r1.at[yd, w, q], s1_send.at[yd, i], s1_recv.at[yd, i], twin
        )

    def s2_copy(yd, part, i):
        w, q = part
        k = lax.rem(y - yd + 4, 4) - 1
        return rcopy(
            s2.at[yd, w, q], r2.at[k, w, q], s2_send.at[yd, i], s2_recv.at[i], (r, xhi * 8 + yd * 2 + core)
        )

    def s2_arrival(part, i):
        w, q = part
        return rcopy(r2.at[:, w, q], r2.at[:, w, q], s2_send.at[0, i], s2_recv.at[i], twin)

    def cut(part, k):
        w, q = part
        n = q.size // 2
        at_once = q.start + jnp.where(k == 1, 0, n)
        later = q.start + jnp.where(k == 1, n, 0)
        return (w, pl.ds(pl.multiple_of(at_once, n), n)), (w, pl.ds(pl.multiple_of(later, n), n))

    def far_copy(yd, part, i, k):
        (w, q), to = cut(part, k)[1], yd + k
        return rcopy(s2.at[yd, w, q], rf.at[w, q], c_send.at[i], f_recv.at[i], y_dev(to))

    def near_copy(yd, part, i, k):
        w, q = part
        return rcopy(s2.at[yd, w, q], r2.at[lax.div(k, 2), w, q], c_send.at[i], c_recv.at[i], y_dev(yd))

    def chain_at(step):
        yd, cd = pair_at(step)
        return yd, cd, lax.rem(y - yd + 4, 4)

    def chain(step, part, i):
        w, q = part
        yd, cd, k = chain_at(step)

        @pl.when(core == cd)
        def _():
            s1_copy(yd, part, i).wait_recv()

            @pl.when(k == 0)
            def _():
                acc[w, q, :] = prod[yd, cd, w, q, :] + r1[yd, w, q, :]

            @pl.when(k == 2)
            def _():
                s2[yd, w, q, :] = (prod[yd, cd, w, q, :] + r1[yd, w, q, :]).astype(BF16)
                far_copy(yd, part, i, 1).start()
                far_copy(yd, part, i, 3).start()

            @pl.when(lax.rem(k, 2) == 1)
            def _():
                h = cut(part, k)[0]
                s2[yd, w, h[1], :] = (prod[yd, cd, w, h[1], :] + r1[yd, w, h[1], :]).astype(BF16)
                near_copy(yd, h, i, k).start()

    def chain_end(step, part, i):
        yd, cd, k = chain_at(step)

        @pl.when(jnp.logical_and(core == cd, lax.rem(k, 2) == 1))
        def _():
            w, q = cut(part, k)[1]
            rcopy(rf.at[w, q], rf.at[w, q], c_send.at[i], f_recv.at[i], twin).wait_recv()
            s2[yd, w, q, :] = (prod[yd, cd, w, q, :] + r1[yd, w, q, :] + rf[w, q, :].astype(F32)).astype(BF16)
            near_copy(yd, (w, q), i, k).start()

    def dot(step, part):
        w, q = part
        yd, cd = pair_at(step)
        queries = pl.ds(pl.multiple_of((2 * yd + cd) * LANES + q.start, BLK), q.size)
        rows = pl.ds(pl.multiple_of(w.start * LANES, LANES), w.size * LANES)
        value = lax.dot_general(
            b_all[queries, :], a_all[rows, :], (((1,), (1,)), ((), ())), preferred_element_type=F32
        )
        for n in range(w.size):
            prod[yd, cd, w.start + n, q, :] = value[:, n * LANES : (n + 1) * LANES]

    def work(step, part, i):
        yd, cd = pair_at(step)
        dot(step, part)

        @pl.when(core != cd)
        def _():
            s1_copy(yd, part, i).start()

    def relay(step, part, i):
        w, q = part
        yd, cd = pair_at(step)

        @pl.when(core == cd)
        def _():
            s1_copy(yd, part, i).wait_recv()

            @pl.when(y == yd)
            def _():
                acc[w, q, :] = prod[yd, cd, w, q, :] + r1[yd, w, q, :]

            @pl.when(y != yd)
            def _():
                s2[yd, w, q, :] = (prod[yd, cd, w, q, :] + r1[yd, w, q, :]).astype(BF16)
                s2_copy(yd, part, i).start()

    def old(step, what):
        def one(g, _):
            what(step, group(4 + g), 2 + g)
            return 0

        lax.fori_loop(0, lax.div(step - 1, 2), one, 0)

    def new(step, what):
        @pl.when(jnp.logical_and(lax.rem(step, 2) == 0, step > 0))
        def _():
            g = lax.div(step, 2) - 1
            if what is work:
                x_group(g).wait_recv()

            def each(t, _):
                what(t, group(4 + g), 2 + g)
                return 0

            lax.fori_loop(1, step + 1, each, 0)

    def newest_copy():
        return rcopy(prod.at[:, 1 - core, 7], r1.at[:, 7], n1_send, n1_recv, twin)

    def newest_on(n):
        yd = lax.rem(y + n, 4)
        return rcopy(
            s2.at[yd, 7], r2.at[3 - n, 7], n2_send, n2_recv, (r, xhi * 8 + yd * 2 + core)
        )

    def newest_all():
        return rcopy(r2.at[:, 7], r2.at[:, 7], n2_send, n2_recv, twin)

    def work_newest():
        x_group(3).wait_recv()
        value = lax.dot_general(
            b_all[...], a_all[pl.ds(7 * LANES, LANES), :], (((1,), (1,)), ((), ())), preferred_element_type=F32
        )
        for j in range(8):
            prod[j // 2, j % 2, 7] = value[j * LANES : (j + 1) * LANES, :]
        newest_copy().start()

    def relay_newest():
        newest_copy().wait_recv()
        for n in (1, 2, 3):
            yd = lax.rem(y + n, 4)
            s2[yd, 7] = (prod[yd, core, 7] + r1[yd, 7]).astype(BF16)
            newest_on(n).start()
        acc[7] = prod[y, core, 7] + r1[y, 7]

    def arrive(step, k):
        for way in range(2):
            chunk = chunk_of(way, k)

            @pl.when(jnp.logical_or(step < NZ // 2, k < NCH // 2))
            def _():
                z_arrival(way, step, chunk).wait_recv()

            @pl.when(jnp.logical_or(step < NZ // 2 - 1, jnp.logical_and(step == NZ // 2 - 1, k < NCH // 2)))
            def _():
                z_copy(way, step + 1, chunk).start()

        if k == 1:
            m_pass(step)

    def follow(step, k):
        i = (step - 1) * NCH + k + XLEAD

        @pl.when(i < NX)
        def _():
            x_copy(i).start()

    own = whole(0, 4)
    most = whole(0, 7)
    first = half(0, 7, soon)
    ends = (half(0, 4, late), half(4, 7, late))

    def body(step, _):
        arrive(step, 0)
        follow(step, 0)

        @pl.when(step > 1)
        def _():
            old(step - 1, work)
            relay(step - 1, own, 0)

        arrive(step, 1)
        follow(step, 1)
        new(step - 1, work)
        arrive(step, 2)
        follow(step, 2)

        @pl.when(step > 1)
        def _():
            old(step - 1, relay)
            z_left(step - 1, BLK)

        new(step - 1, relay)

        for phase in (1, 2, 3):
            @pl.when(step == phase)
            def _():
                norms(phase)

        arrive(step, 3)
        follow(step, 3)

        @pl.when(step < last - 1)
        def _():
            work(step, own, 0)

        return 0

    lax.fori_loop(1, last, body, 0)

    yd7, cd7 = pair_at(last - 1)
    yd8, cd8 = pair_at(last)
    at7 = pl.ds(pl.multiple_of((2 * yd7 + cd7) * LANES, LANES), LANES)
    at8 = pl.ds(pl.multiple_of((2 * yd8 + cd8) * LANES + soon, BLK), BLK)
    value = lax.dot_general(
        jnp.concatenate([b_all[at7, :], b_all[at8, :]], axis=0), a_all[pl.ds(0, 7 * LANES), :],
        (((1,), (1,)), ((), ())), preferred_element_type=F32,
    )
    for n in range(7):
        prod[yd7, cd7, n] = value[:LANES, n * LANES : (n + 1) * LANES]
        prod[yd8, cd8, n, first[1], :] = value[LANES:, n * LANES : (n + 1) * LANES]
    for step, part in ((last - 1, most), (last, first)):
        @pl.when(core != pair_at(step)[1])
        def _():
            s1_copy(pair_at(step)[0], part, 0).start()

    @pl.when(2 * y + core == pair_of(z, last - 1))
    def _():
        r2[2, most[0], most[1], :] = jnp.zeros((7, LANES, LANES), BF16)

    @pl.when(2 * y + core == pair_of(z, last))
    def _():
        r2[2, first[0], first[1], :] = jnp.zeros((7, BLK, LANES), BF16)

    arrive(last, 0)
    chain(last - 1, most, 0)
    chain(last, first, 0)
    arrive(last, 1)
    work(last, ends[0], 1)
    send_shares()
    chain_end(last - 1, most, 0)
    chain_end(last, first, 0)
    work(last, ends[1], 2)
    relay(last, ends[0], 1)
    relay(last, ends[1], 2)
    work_newest()
    relay_newest()

    j_last, j_before = pair_of(z, last), pair_of(z, last - 1)
    of_chain = ([(first, 0)], [(most, 0)], [])
    of_own = ([(ends[0], 1)], [], [(own, 0)])
    of_old = ([(ends[1], 2)], [], [(group(4 + g), 2 + g) for g in range(3)])

    def by_pair(j, cases, do):
        is_one, is_two = j == j_last, j == j_before
        tests = (is_one, is_two, jnp.logical_not(jnp.logical_or(is_one, is_two)))
        for test, some in zip(tests, cases):
            if some:
                @pl.when(test)
                def _():
                    for part, i in some:
                        do(part, i)

    def c_arrival(part, i):
        w, q = part
        two = r2.at[pl.ds(0, 2), w, q]
        return rcopy(two, two, c_send.at[i], c_recv.at[i], twin)

    def y_arrived(cases):
        by_pair(2 * y + core, cases, lambda part, i: s2_arrival(part, i).wait_recv())

    def summed(w):
        return acc[w] + r2[0, w].astype(F32) + r2[1, w].astype(F32) + r2[2, w].astype(F32)

    def s3_own(u):
        return rcopy(sx.at[u], rx.at[0, u], s3_send.at[u], s3_recv.at[0, u], xhop)

    def s3_pair(u):
        return rcopy(sx.at[4 + u], rx.at[0, u], s3_send.at[4 + u], s3_recv.at[0, u], xpair)

    def s3_diag(u):
        return rcopy(sx.at[4 + u], rx.at[1, u], s3_send.at[4 + u], s3_recv.at[1, u], diag)

    by_pair(2 * y + core, of_chain, lambda part, i: c_arrival(part, i).wait_recv())
    y_arrived(of_own)
    for u in range(4):
        total = summed(u)

        @pl.when(home)
        def _():
            keep[u] = total

        @pl.when(jnp.logical_not(home))
        def _():
            sx[u] = total.astype(BF16)
            s3_own(u).start()

    for u in range(4):
        if u == 0:
            y_arrived(of_old)
        if u == 3:
            newest_all().wait_recv()
        sx[4 + u] = summed(4 + u).astype(BF16)

        @pl.when(home)
        def _():
            s3_pair(u).start()

        @pl.when(jnp.logical_not(home))
        def _():
            s3_diag(u).start()

    sum_shares()

    def left(yd, _):
        def out(copy, j):
            by_pair(
                j, [a + b + d for a, b, d in zip(of_chain, of_own, of_old)],
                lambda part, i: copy(yd, part, i).wait_send(),
            )

        def chained(yd, part, i):
            w, q = part
            return rcopy(s2.at[yd, w, q], s2.at[yd, w, q], c_send.at[i], c_recv.at[i], twin)

        def passed(j):
            by_pair(j, of_chain, lambda part, i: chained(yd, part, i).wait_send())
            by_pair(
                j, [a + b for a, b in zip(of_own, of_old)], lambda part, i: s2_copy(yd, part, i).wait_send()
            )

        out(s1_copy, 2 * yd + 1 - core)

        @pl.when(yd != y)
        def _():
            passed(2 * yd + core)

        return 0

    lax.fori_loop(0, 4, left, 0)
    z_left(last - 1, BLK)
    z_left(last, BLK // 2)
    for g in range(4):
        x_group(g).wait_send()
    for k in range(5):
        t_copy(k).wait_send()
    newest_copy().wait_send()
    newest_all().wait_send()
    for way in range(2):
        gone = metas.at[pl.ds(0, NZ // 2 - way)]
        rcopy(gone, gone, m_send.at[way], m_recv.at[way, 0], up).wait_send()

    @pl.when(home)
    def _():
        q_sent(7).wait_send()
        m_pair().wait_send()

    @pl.when(jnp.logical_not(home))
    def _():
        q_sent(8).wait_send()

    @pl.when(jnp.logical_not(home))
    def _():
        m_pair().wait_recv()

    lane = lax.broadcasted_iota(jnp.int32, (8, LANES), 1)
    both = jnp.where(lane < BLK, mpair[0], pltpu.roll(mpair[1], BLK, 1))
    q_inv = jnp.broadcast_to(1.0 / jnp.sqrt(both[0:1, :] + EPS), (LANES, LANES)).T
    q_ids = jnp.broadcast_to(both[1:2, :], (LANES, LANES)).T
    t_ids = tid_ref[...].astype(F32)

    ppart[...] = jnp.zeros_like(ppart)
    for u in range(4):
        s3_pair(u).wait_recv()

        @pl.when(jnp.logical_not(home))
        def _():
            s3_diag(u).wait_recv()
            keep[u] = rx[1, u].astype(F32)

        raw = keep[u] + rx[0, u].astype(F32)
        value = raw * q_inv * tinv[u : u + 1, :]
        value = jnp.where(q_ids == t_ids[u : u + 1, :], 0.0, value)
        ppart[u : u + 1, :] = jnp.max(value, axis=0, keepdims=True)
        cos_ref[u] = value

    def send_peaks(k, _):
        to_col(ppart, peaks, p_send, p_recv, k).start()
        return 0

    lax.fori_loop(1, 16, send_peaks, 0)
    peaks[c] = ppart[...]
    for u in range(4):
        @pl.when(jnp.logical_not(home))
        def _():
            s3_own(u).wait_send()

        s3_pair(u).wait_send()

    all_of_col(peaks, p_send, p_recv).wait()


def lay_out(tiles, peaks, cos_ref, peak_ref):
    for u in range(4):
        cos_ref[pl.ds(u * LANES, LANES), :] = tiles[u].T
    best = peaks[0]
    for k in range(1, 16):
        best = jnp.maximum(best, peaks[k])
    peak_ref[...] = best[0:4, :]


def shards(train_codes, train_exps, train_ids, query_codes, query_exps, query_ids, precond):
    dma = pltpu.SemaphoreType.DMA
    vmem = pl.BlockSpec(memory_space=pltpu.VMEM)
    hbm = pl.BlockSpec(memory_space=pl.ANY)
    tiles, peaks = pl.pallas_call(
        kernel,
        out_shape=(pltpu.VMEM((4, LANES, LANES), F32), pltpu.VMEM((16, 8, LANES), F32)),
        in_specs=[hbm] * 7,
        out_specs=(vmem, vmem),
        scratch_shapes=[
            pltpu.VMEM((ROWS, KD), BF16),
            pltpu.VMEM((NBLK, ROWS), jnp.int32),
            pltpu.VMEM((ROWS, NBLK), F32),
            pltpu.VMEM((4, LANES), jnp.int32),
            pltpu.VMEM((BLK, KD), BF16),
            pltpu.VMEM((NBLK, BLK), jnp.int32),
            pltpu.VMEM((1, BLK), jnp.int32),
            pltpu.VMEM((NBLK, LANES), F32),
            pltpu.VMEM((2 * ROWS, KD), BF16),
            pltpu.VMEM((NZ * BLK, KD), BF16),
            pltpu.VMEM((ROWS, LANES), F32),
            pltpu.VMEM((4, 2, 8, LANES, LANES), F32),
            pltpu.VMEM((4, 8, LANES, LANES), F32),
            pltpu.VMEM((4, 8, LANES, LANES), BF16),
            pltpu.VMEM((3, 8, LANES, LANES), BF16),
            pltpu.VMEM((8, LANES, LANES), BF16),
            pltpu.VMEM((8, LANES, LANES), F32),
            pltpu.VMEM((8, LANES, LANES), BF16),
            pltpu.VMEM((2, 4, LANES, LANES), BF16),
            pltpu.VMEM((4, LANES, LANES), F32),
            pltpu.VMEM((8, LANES), F32),
            pltpu.VMEM((5, 8, LANES), F32),
            pltpu.VMEM((2, 8, LANES), F32),
            pltpu.VMEM((NZ, 8, LANES), F32),
            pltpu.VMEM((16, 2, 8, LANES), F32),
            pltpu.VMEM((2, 8, LANES), F32),
            pltpu.VMEM((2, 8, LANES), F32),
            pltpu.VMEM((8, LANES), F32),
            pltpu.VMEM((8, LANES), F32),
            dma((NIN + 6,)),
            dma((2, NZ // 2 + 1)), dma((2, NZ // 2 + 1, NCH)),
            dma((4,)), dma((4,)),
            dma((4, 5)), dma((4, 5)),
            dma((4, 5)), dma((5,)),
            dma((1,)), dma((1,)), dma((1,)),
            dma, dma, dma, dma,
            dma((8,)), dma((2, 4)),
            dma((5,)), dma((5,)),
            dma((2,)), dma((2, NZ // 2 + 1)), dma, dma, dma, dma,
            dma, dma,
        ],
        compiler_params=pltpu.CompilerParams(
            collective_id=0, has_side_effects=True, vmem_limit_bytes=VMEM
        ),
        cost_estimate=pl.CostEstimate(
            flops=2 * ROWS * 2048 * KD, bytes_accessed=3 * 2**20, transcendentals=0
        ),
    )(
        train_codes, train_exps.T, train_ids.reshape(4, LANES), query_codes, query_exps.T,
        query_ids.reshape(1, BLK), precond.reshape(NBLK, LANES),
    )
    cosines, peak = pl.pallas_call(
        lay_out,
        out_shape=(jax.ShapeDtypeStruct((ROWS, LANES), F32), jax.ShapeDtypeStruct((4, LANES), F32)),
        in_specs=[vmem, vmem],
        out_specs=(vmem, vmem),
    )(tiles, peaks)
    return cosines, peak.reshape(ROWS)


def solution(mesh):
    in_specs = (
        P("row", "col"),
        P("row", "col"),
        P("row"),
        P("row", "col"),
        P("row", "col"),
        P("row"),
        P("col"),
    )
    out_specs = (P("row", "col"), P("row"))
    return jax.shard_map(shards, mesh=mesh, in_specs=in_specs, out_specs=out_specs, check_vma=False)
```
